256 devices in a mesh: freq: 4 (over x_hi, core), strip: 64 (over x_lo, z, y).
Axes of the slice: x: 4 (x_hi: 2, x_lo: 2; x = x_hi * 2 + x_lo), y: 4, z: 8, core: 2. Of those that a mesh axis runs over, the one named last changes fastest.
Arguments:
- source: float32 [2, 4, 512, 8192], P(None, 'freq', None, 'strip'), may hold values from -6 to 6
- receiver: float32 [2, 4, 512, 8192], P(None, 'freq', None, 'strip'), may hold values from -6 to 6
- velocity: float32 [2, 512, 8192], P(None, 'strip'), may hold values from 1.5 to 4.5
- omega: float32 [4], P('freq'), may hold values from 1 to 3
Outputs:
- image: float32 [2, 512, 8192], P(None, 'freq', 'strip')
The draws below stay inside these ranges and needn't reach their ends.
All inputs are finite; a program needn't handle non-finite values.
Results may differ from the reference program's by a relative error of at most 0.00002.
Values sent between devices are 32-bit elements; how exact they have to be, the bound alone decides.
No kernel may reach another device: no remote copies, remote signals or barrier semaphores. Data moves between devices by JAX's collectives and lax.ppermute only.
A program may use at most 64 MiB of HBM per device.

```python
import math
import jax
import jax.numpy as jnp
from jax import lax

NX = 512
DEPTHS = 2
SUBS = 2
NY = 8192
FREQS = 4


def block_scale(stream_key, dims, shards, least, largest):
    def one(dim, parts):
        steps = jax.random.uniform(jax.random.fold_in(jax.random.fold_in(stream_key, 6), dim), (parts,), jnp.float32, least / len(shards), largest / len(shards))
        return jnp.repeat(jnp.exp(steps), dims[dim] // parts).reshape((-1,) + (1,) * (len(dims) - dim - 1))

    loudness = one(*shards[0])
    for cut in shards[1:]:
        loudness = loudness * one(*cut)
    return loudness


def normal_values(own_key, shape, spread, limit, pieces=(), held_as=jnp.bfloat16):
    result = jax.random.normal(own_key, shape, jnp.float32) * spread
    if len(pieces) > 0:
        result = block_scale(own_key, shape, pieces, -0.22, 0.18) * result
    return jnp.clip(result, min=-limit, max=limit).astype(held_as)


def setup_inputs(seed: int = 0) -> dict:
    arg_keys = jax.random.split(jax.random.key(seed), 5)
    source = normal_values(arg_keys[0], (2, FREQS, NX, NY), 1.0, 6.0, ((1, 4), (3, 64)), jnp.float32)
    receiver = normal_values(arg_keys[1], (2, FREQS, NX, NY), 1.0, 6.0, ((1, 4), (3, 64)), jnp.float32)
    velocity = jnp.clip(1.5 + 3.0 * jax.random.uniform(arg_keys[2], (DEPTHS, NX, NY), jnp.float32) ** block_scale(arg_keys[2], (DEPTHS, NX, NY), ((1, 64),), -0.2, 0.2), 1.5, 4.5)
    omega = jnp.clip(jnp.exp(math.log(3.0) - 1.0986123 * jax.random.uniform(arg_keys[3], (FREQS,), jnp.float32) ** block_scale(arg_keys[3], (FREQS,), ((0, 4),), -0.2, 0.2)), 1.0, 3.0)
    return dict(source=source, receiver=receiver, velocity=velocity, omega=omega)


phase_depth = 2.0
fd_coef = 0.03


def laplace(field):
    padded = jnp.pad(field, ((1, 1), (1, 1)))
    beside_all = padded[2:, 1:-1] + padded[:-2, 1:-1] + padded[1:-1, 2:] + padded[1:-1, :-2]
    return beside_all - 4.0 * field


def extrapolate(real, imag, speed, freq, sign):
    theta = sign * freq * phase_depth / speed
    cosine = jnp.cos(theta)
    sine = jnp.sin(theta)
    real, imag = real * cosine - imag * sine, real * sine + imag * cosine
    coef = sign * fd_coef * speed / freq
    for sub in range(SUBS):
        lap_real = laplace(real)
        lap_imag = laplace(imag)
        real, imag = real - coef * lap_imag, imag + coef * lap_real
    return real, imag


def reference(source, receiver, velocity, omega):
    def one_freq(image, index):
        src_re = source[0][index]
        src_im = source[1][index]
        rec_re = receiver[0][index]
        rec_im = receiver[1][index]
        freq = omega[index]
        layers = []
        for depth in range(DEPTHS):
            speed = velocity[depth]
            src_re, src_im = extrapolate(src_re, src_im, speed, freq, 1.0)
            rec_re, rec_im = extrapolate(rec_re, rec_im, speed, freq, -1.0)
            layers.append(src_re * rec_re + src_im * rec_im)
        return image + jnp.stack(layers), None

    start = jnp.zeros((DEPTHS, NX, NY), jnp.float32)
    image, unused = lax.scan(one_freq, start, jnp.arange(FREQS, dtype=jnp.int32))
    return image
```

```python
import functools

import jax
import jax.numpy as jnp
from jax import lax
from jax.experimental import pallas as pl
from jax.experimental.pallas import tpu as pltpu
from jax.sharding import PartitionSpec as P

FREQS = 4
LANES = 128
TILE = 8
WIN = 32
HALO = 4
CORE_ROWS = 128
ROWS = CORE_ROWS + 2 * TILE
GUARD = TILE
CHUNK = 48

phase_depth = 2.0
fd_coef = 0.03

F32 = jnp.float32


def lanes_of(rows):
    return lax.broadcasted_iota(jnp.int32, (rows, LANES), 1)


def lane_roll(x, shift):
    return pltpu.roll(x, shift % LANES, 1)


def pack_speed(vel_ref, out_ref):
    strips = vel_ref.shape[2] // LANES
    lane = lanes_of(TILE)
    sublane = lax.broadcasted_iota(jnp.int32, (TILE, LANES), 0)
    for strip in range(strips):
        base = 17 * strip
        after = min(strip + 1, strips - 1)
        before = max(strip - 1, 0)
        beside = jnp.zeros((TILE, LANES), F32)
        for depth in range(2):
            here = vel_ref[depth, :, strip * LANES : (strip + 1) * LANES]
            out_ref[base + depth * TILE : base + (depth + 1) * TILE, :] = here
            right = vel_ref[depth, :, after * LANES : (after + 1) * LANES]
            left = vel_ref[depth, :, before * LANES : (before + 1) * LANES]
            start = depth * 2 * HALO
            right = lane_roll(right, start) if depth else right
            left = lane_roll(left, start + 2 * HALO)
            beside = jnp.where((lane >= start) & (lane < start + HALO), right, beside)
            beside = jnp.where(
                (lane >= start + HALO) & (lane < start + 2 * HALO), left, beside
            )
        for shift in (16, 32, 64):
            beside = beside + lane_roll(beside, shift)
        beside = jnp.where(lane // 16 == 7 - sublane, beside, 0.0)
        out_ref[base + 16 : base + 17, :] = jnp.sum(beside, axis=0, keepdims=True)


def prepare(src_ref, rec_ref, *outs):
    messages, own_ref, to_left_ref, to_right_ref = outs[:FREQS], outs[4], outs[5], outs[6]
    fields = (src_ref.at[0, 0], src_ref.at[1, 0], rec_ref.at[0, 0], rec_ref.at[1, 0])
    freq = lax.axis_index("freq")
    rows = src_ref.shape[2]
    for k in range(FREQS):
        block = freq ^ k
        mid = pl.multiple_of(block * CORE_ROWS, CORE_ROWS)
        above = pl.multiple_of(jnp.maximum(mid - TILE, 0), TILE)
        below = pl.multiple_of(jnp.minimum(mid + CORE_ROWS, rows - TILE), TILE)
        for part, field in enumerate(fields):
            out = messages[k].at[part]
            out[TILE : TILE + CORE_ROWS, :] = field[pl.ds(mid, CORE_ROWS), :]
            out[0:TILE, :] = jnp.where(block > 0, field[pl.ds(above, TILE), :], 0.0)
            out[TILE + CORE_ROWS : ROWS, :] = jnp.where(
                block < FREQS - 1, field[pl.ds(below, TILE), :], 0.0
            )
    groups = rows // 64
    lane = lanes_of(64)
    place = lane % WIN
    to_left = jnp.zeros((64, LANES), F32)
    to_right = jnp.zeros((64, LANES), F32)
    for q in range(groups):
        edge = jnp.zeros((64, LANES), F32)
        for part, field in enumerate(fields):
            value = field[q * 64 : (q + 1) * 64, :]
            mine = lane // WIN == part
            edge = jnp.where(
                mine & (place >= 4) & (place < 16), lane_roll(value, part * WIN + 4), edge
            )
            edge = jnp.where(
                mine & (place >= 16) & (place < 28), lane_roll(value, part * WIN + 28), edge
            )
        own_ref[q * 64 : (q + 1) * 64, :] = edge
        slot = place // HALO == q
        to_left = jnp.where(slot, lane_roll(edge, HALO * q - 4), to_left)
        to_right = jnp.where(slot, lane_roll(edge, HALO * q - 24), to_right)
    to_left_ref[...] = to_left
    to_right_ref[...] = to_right


def join_edges(own_ref, left_ref, right_ref, omega_ref, *outs):
    messages, full = outs[:FREQS], outs[FREQS]
    freq = lax.axis_index("freq")
    rows = own_ref.shape[0]
    lane = lanes_of(64)
    place = lane % WIN
    full[0:TILE, :] = jnp.zeros((TILE, LANES), F32)
    full[TILE + rows :, :] = jnp.zeros((TILE, LANES), F32)
    left = left_ref[...]
    right = right_ref[...]
    for q in range(rows // 64):
        edge = own_ref[q * 64 : (q + 1) * 64, :]
        edge = jnp.where(place < 4, lane_roll(left, -HALO * q), edge)
        edge = jnp.where(place >= 28, lane_roll(right, 28 - HALO * q), edge)
        full[TILE + q * 64 : TILE + (q + 1) * 64, :] = edge
    for k in range(FREQS):
        start = pl.multiple_of((freq ^ k) * CORE_ROWS, CORE_ROWS)
        messages[k][0:ROWS, :] = full[pl.ds(start, ROWS), :]
        messages[k][ROWS : ROWS + TILE, :] = jnp.full((TILE, LANES), omega_ref[0], F32)


def sin_cos(x):
    turns = jnp.round(x * 0.6366197723675814)
    r = x - turns * 1.5703125
    r = r - turns * 4.837512969970703125e-4
    r = r - turns * 7.54978995489188216e-8
    square = r * r
    sine = r + r * square * (
        -1.6666654611e-1 + square * (8.3321608736e-3 + square * -1.9515295891e-4)
    )
    cosine = (
        1.0
        - 0.5 * square
        + square
        * square
        * (
            4.166664568298827e-2
            + square * (-1.388731625493765e-3 + square * 2.443315711809948e-5)
        )
    )
    quarter = turns.astype(jnp.int32)
    odd = (quarter & 1) == 1
    out_sin = jnp.where(odd, cosine, sine)
    out_cos = jnp.where(odd, sine, cosine)
    out_sin = jnp.where((quarter & 2) == 2, -out_sin, out_sin)
    out_cos = jnp.where(((quarter + 1) & 2) == 2, -out_cos, out_cos)
    return out_sin, out_cos


def march(*refs):
    speed_ref = refs[0]
    mains = refs[1:5]
    edges = refs[5:9]
    image_ref = refs[9]
    waves, speed, coef, omega, first, second = refs[10:]
    freq = lax.axis_index("freq")
    strip = lax.axis_index("strip")
    strips = lax.axis_size("strip")
    lane = lanes_of(TILE)
    place = lane % WIN

    block_rows = 17 * (CORE_ROWS // TILE)
    mid = pl.multiple_of(freq * block_rows, TILE)
    above = pl.multiple_of(jnp.maximum(mid - 24, 0), TILE)
    below = pl.multiple_of(jnp.minimum(mid + block_rows, speed_ref.shape[0] - 24), TILE)
    stage = omega.at[pl.ds(TILE * 5, 320), :]
    stage[0:24, :] = speed_ref[pl.ds(above, 24), :]
    stage[24 : 24 + block_rows, :] = speed_ref[pl.ds(mid, block_rows), :]
    stage[24 + block_rows : 48 + block_rows, :] = speed_ref[pl.ds(below, 24), :]
    blocks = CORE_ROWS // TILE + 2
    off_left = (place < 4) & (strip == 0)
    off_right = (place >= 28) & (strip == strips - 1)
    inside = jnp.logical_not(off_left | off_right)
    for i in range(blocks):
        base = 7 + 17 * i
        beside = jnp.broadcast_to(stage[base + 16 : base + 17, :], (TILE, LANES))
        beside = pltpu.roll(beside, 0, 1, stride=16, stride_axis=0)
        live = True
        if i == 0:
            live = freq > 0
        elif i == blocks - 1:
            live = freq < FREQS - 1
        for depth in range(2):
            here = stage[base + depth * TILE : base + (depth + 1) * TILE, :]
            halo = lane_roll(beside, 28 - 112 - 2 * HALO * depth)
            window = jnp.where((lane >= 28) & (lane < 36), halo, 0.0)
            window = jnp.where((lane >= 4) & (lane < 16), lane_roll(here, 4), window)
            window = jnp.where((lane >= 16) & (lane < 28), lane_roll(here, 28), window)
            window = window + lane_roll(window, WIN)
            window = window + lane_roll(window, 2 * WIN)
            rows = slice(i * TILE, (i + 1) * TILE)
            speed[0, depth, rows, :] = phase_depth / here
            speed[1, depth, rows, :] = phase_depth / window
            main_coef = fd_coef * here
            edge_coef = jnp.where(inside, fd_coef * window, 0.0)
            if live is not True:
                main_coef = jnp.where(live, main_coef, 0.0)
                edge_coef = jnp.where(live, edge_coef, 0.0)
            coef[0, depth, rows, :] = main_coef
            coef[1, depth, rows, :] = edge_coef

    lane_omega = jnp.zeros((TILE, LANES), F32)
    for k in range(FREQS):
        row = edges[k][ROWS : ROWS + TILE, :]
        omega[k * TILE : (k + 1) * TILE, :] = row
        lane_omega = jnp.where(lane // WIN == k, row, lane_omega)
        waves[k] = mains[k][...]
    omega[FREQS * TILE : (FREQS + 1) * TILE, :] = lane_omega
    for i in range(ROWS // TILE):
        rows = slice(i * TILE, (i + 1) * TILE)
        for part in range(4):
            value = jnp.zeros((TILE, LANES), F32)
            for k in range(FREQS):
                piece = edges[k][rows, :]
                value = jnp.where(
                    lane // WIN == k, lane_roll(piece, (k - part) * WIN), value
                )
            waves[FREQS, part, rows, :] = value

    guard = jnp.zeros((TILE, LANES), F32)
    for buffer in (first, second):
        for part in range(4):
            buffer[part, 0:GUARD, :] = guard
            buffer[part, GUARD + ROWS :, :] = guard
    image_ref[...] = jnp.zeros_like(image_ref)

    chunks = ROWS // CHUNK

    def turn(values, depth, kind, row, freq_row):
        theta = freq_row * speed[kind, depth, pl.ds(row, CHUNK), :]
        sine, cosine = sin_cos(theta)
        src_re, src_im, rec_re, rec_im = values
        return (
            src_re * cosine - src_im * sine,
            src_re * sine + src_im * cosine,
            rec_re * cosine + rec_im * sine,
            rec_im * cosine - rec_re * sine,
        )

    def substep(buffer, depth, kind, row, freq_inverse):
        step = coef[kind, depth, pl.ds(row, CHUNK), :] * freq_inverse
        centers = []
        laps = []
        for part in range(4):
            center = buffer[part, pl.ds(row + GUARD, CHUNK), :]
            up = buffer[part, pl.ds(row + GUARD - 1, CHUNK), :]
            down = buffer[part, pl.ds(row + GUARD + 1, CHUNK), :]
            across = lane_roll(center, 1) + lane_roll(center, LANES - 1)
            centers.append(center)
            laps.append((across + (up + down)) - 4.0 * center)
        src_re, src_im, rec_re, rec_im = centers
        return (
            src_re - step * laps[1],
            src_im + step * laps[0],
            rec_re + step * laps[3],
            rec_im - step * laps[2],
        )

    def store(buffer, row, values):
        for part in range(4):
            buffer[part, pl.ds(row + GUARD, CHUNK), :] = values[part]

    def product(values):
        return values[0] * values[2] + values[1] * values[3]

    def item(k, kind, add_image):
        freq_row = omega[pl.ds(pl.multiple_of(k * TILE, TILE), 1), :]
        freq_inverse = 1.0 / freq_row

        for j in range(chunks):
            row = j * CHUNK
            values = [waves[k, part, pl.ds(row, CHUNK), :] for part in range(4)]
            store(first, row, turn(values, 0, kind, row, freq_row))
        for j in range(chunks):
            store(second, j * CHUNK, substep(first, 0, kind, j * CHUNK, freq_inverse))
        for j in range(chunks):
            row = j * CHUNK
            values = substep(second, 0, kind, row, freq_inverse)
            add_image(0, row, product(values))
            store(first, row, turn(values, 1, kind, row, freq_row))
        for j in range(chunks):
            store(second, j * CHUNK, substep(first, 1, kind, j * CHUNK, freq_inverse))
        for j in range(chunks):
            values = substep(second, 1, kind, j * CHUNK, freq_inverse)
            add_image(1, j * CHUNK, product(values))

    def cut(row):
        low = max(row, TILE)
        high = min(row + CHUNK, TILE + CORE_ROWS)
        return low, high

    def add_main(depth, row, value):
        low, high = cut(row)
        image_ref[depth, low - TILE : high - TILE, :] += value[low - row : high - row, :]

    def patch(depth, row, value):
        low, high = cut(row)
        value = value[low - row : high - row, :]
        value = value + lane_roll(value, WIN)
        value = value + lane_roll(value, 2 * WIN)
        wide = lanes_of(high - low)
        old = image_ref[depth, low - TILE : high - TILE, :]
        new = jnp.where(wide < HALO, lane_roll(value, -4), old)
        new = jnp.where(wide >= LANES - HALO, lane_roll(value, 4), new)
        image_ref[depth, low - TILE : high - TILE, :] = new

    def one_freq(k, carry):
        item(k, 0, add_main)
        return carry

    lax.fori_loop(0, FREQS, one_freq, 0)
    item(FREQS, 1, patch)


def shape(*dims):
    return jax.ShapeDtypeStruct(dims, F32)


def shards(source, receiver, velocity, omega):
    strips = lax.axis_size("strip")
    rows = source.shape[2]
    vmem = pl.BlockSpec(memory_space=pltpu.VMEM)
    smem = pl.BlockSpec(memory_space=pltpu.SMEM)

    packed = pl.pallas_call(
        pack_speed, out_shape=shape(17 * strips, LANES), in_specs=[vmem], out_specs=vmem
    )(velocity)
    speeds = lax.all_to_all(
        packed.reshape(strips, 1, 17 * LANES), "strip", split_axis=0, concat_axis=0, tiled=True
    ).reshape(17 * strips, LANES)

    prepared = pl.pallas_call(
        prepare,
        out_shape=[shape(4, ROWS, LANES)] * FREQS
        + [shape(rows, LANES), shape(64, LANES), shape(64, LANES)],
        in_specs=[vmem, vmem],
        out_specs=[vmem] * 7,
    )(source, receiver)
    mains, own, to_left, to_right = prepared[:FREQS], prepared[4], prepared[5], prepared[6]

    def across(x, k):
        return lax.ppermute(x, "freq", [(i, i ^ k) for i in range(FREQS)])

    from_left = lax.ppermute(to_right, "strip", [(i, i + 1) for i in range(strips - 1)])
    from_right = lax.ppermute(to_left, "strip", [(i + 1, i) for i in range(strips - 1)])
    mains = [mains[0]] + [across(mains[k], k) for k in range(1, FREQS)]
    edges = pl.pallas_call(
        join_edges,
        out_shape=[shape(ROWS + TILE, LANES)] * FREQS,
        in_specs=[vmem, vmem, vmem, smem],
        out_specs=[vmem] * FREQS,
        scratch_shapes=[pltpu.VMEM((rows + 2 * TILE, LANES), F32)],
    )(own, from_left, from_right, omega)
    edges = [edges[0]] + [across(edges[k], k) for k in range(1, FREQS)]

    return pl.pallas_call(
        march,
        out_shape=shape(2, CORE_ROWS, LANES),
        in_specs=[vmem] * 9,
        out_specs=vmem,
        scratch_shapes=[
            pltpu.VMEM((FREQS + 1, 4, ROWS, LANES), F32),
            pltpu.VMEM((2, 2, ROWS, LANES), F32),
            pltpu.VMEM((2, 2, ROWS, LANES), F32),
            pltpu.VMEM((5 * TILE + 320, LANES), F32),
            pltpu.VMEM((4, ROWS + 2 * GUARD, LANES), F32),
            pltpu.VMEM((4, ROWS + 2 * GUARD, LANES), F32),
        ],
    )(speeds, *mains, *edges)


def solution(mesh):
    return jax.shard_map(
        shards,
        mesh=mesh,
        in_specs=(
            P(None, "freq", None, "strip"),
            P(None, "freq", None, "strip"),
            P(None, "strip", None),
            P("freq"),
        ),
        out_specs=P(None, "freq", "strip"),
        check_vma=False,
    )
```

```python
import functools

import jax
import jax.numpy as jnp
from jax import lax
from jax.experimental import pallas as pl
from jax.experimental.pallas import tpu as pltpu
from jax.sharding import PartitionSpec as P

BLOCKS = 4
ITEMS = 4
LANES = 128
TILE = 8
WIN = 32
HALO = 4
CORE_ROWS = 128
ROWS = CORE_ROWS + 2 * TILE
GUARD = TILE
CHUNK = 72
SPAN = 9

phase_depth = 2.0
fd_coef = 0.03

F32 = jnp.float32


def lanes_of(rows):
    return lax.broadcasted_iota(jnp.int32, (rows, LANES), 1)


def lane_roll(x, shift):
    return pltpu.roll(x, shift % LANES, 1)


def pack_speed(vel_ref, out_ref, held, sem):
    core = lax.axis_index("freq") & 1
    copy = pltpu.make_async_copy(vel_ref.at[core], held, sem)
    copy.start()
    strips = vel_ref.shape[2] // LANES
    group = 16
    dims = (group, TILE, LANES)
    lane = lax.broadcasted_iota(jnp.int32, dims, 2)
    sublane = lax.broadcasted_iota(jnp.int32, dims, 1)
    copy.wait()

    def one_group(step, carry):
        def strip_of(i):
            strip = jnp.clip(step * group + i, 0, strips - 1)
            return held[:, pl.ds(pl.multiple_of(strip * LANES, LANES), LANES)]

        span = [strip_of(i) for i in range(-1, group + 1)]
        left = pltpu.roll(jnp.stack(span[:group]), 2 * HALO, 2)
        beside = jnp.where(lane < HALO, jnp.stack(span[2:]), left)
        beside = jnp.where(lane < 2 * HALO, beside, 0.0)
        for shift in (16, 32, 64):
            beside = beside + pltpu.roll(beside, shift, 2)
        beside = jnp.where((lane >> 4) == 7 - sublane, beside, 0.0)
        beside = jnp.sum(beside, axis=1, keepdims=True)
        out = out_ref.at[pl.ds(pl.multiple_of(step * group * SPAN, TILE), group * SPAN)]
        for i in range(group):
            out[SPAN * i : SPAN * i + TILE, :] = span[i + 1]
            out[SPAN * i + TILE : SPAN * (i + 1), :] = beside[i]
        return carry

    lax.fori_loop(0, strips // group, one_group, 0)


def first_row(block, rows):
    start = jnp.clip(block * CORE_ROWS - TILE, 0, rows - ROWS)
    return pl.multiple_of(start, TILE)


def cut_waves(src_ref, rec_ref, edges_ref, message_ref):
    other = 1 - (lax.axis_index("freq") & 1)
    fields = (src_ref.at[0, 0], src_ref.at[1, 0], rec_ref.at[0, 0], rec_ref.at[1, 0])
    lane = lanes_of(CORE_ROWS)
    packed = jnp.zeros((CORE_ROWS, LANES), F32)
    for group in range(BLOCKS):
        for part, field in enumerate(fields):
            slot = 4 * group + part
            value = field[group * CORE_ROWS : (group + 1) * CORE_ROWS, :]
            packed = jnp.where((lane >> 3) == slot, lane_roll(value, 8 * slot + 4), packed)
    edges_ref[...] = jnp.where((lane & 7) < 4, lane_roll(packed, -4), lane_roll(packed, 4))
    for b in range(2):
        rows = pl.ds(first_row(2 * b + other, src_ref.shape[2]), ROWS)
        for part, field in enumerate(fields):
            message_ref[4 * b + part] = field[rows, :]


SIN_TERMS = (1.0, -0.166666641831398, 0.008333218283951283, -0.00019823516777250916, 2.643730113049969e-06)
COS_TERMS = (1.0, -0.5, 0.041666656732559204, -0.0013888673856854439, 2.4778757506283e-05, -2.6437069777784927e-07)


def horner(terms, x):
    value = terms[-1]
    for term in terms[-2::-1]:
        value = value * x + term
    return value


def sin_cos(x):
    t = 0.5 * x - 0.7853981633974483
    square = t * t
    sine = t * horner(SIN_TERMS, square)
    cosine = horner(COS_TERMS, square)
    twice = -2.0 * sine
    return 1.0 + twice * sine, twice * cosine


def march(*refs):
    speed_refs, src_ref, rec_ref, message_ref, halo_refs = refs[:2], *refs[2:5], refs[5:7]
    own_ref, send_ref = refs[7:9]
    waves, sides, stage, speed, coef, omega, first, second, images, sems = refs[9:]
    freq = lax.axis_index("freq")
    core = freq & 1
    strip = lax.axis_index("strip")
    strips = lax.axis_size("strip")
    copies = []

    def copy_in(source, target):
        copy = pltpu.make_async_copy(source, target, sems.at[len(copies)])
        copy.start()
        copies.append(copy)

    block_rows = SPAN * (CORE_ROWS // TILE)
    for b in range(2):
        mid = pl.multiple_of((2 * b + core) * block_rows, TILE)
        above = pl.multiple_of(jnp.maximum(mid - 16, 0), TILE)
        below = pl.multiple_of(jnp.minimum(mid + block_rows, strips * SPAN - 16), TILE)
        for which, speed_ref in enumerate(speed_refs):
            target = stage.at[core ^ which, b]
            copy_in(speed_ref.at[pl.ds(above, 16)], target.at[0:16])
            copy_in(speed_ref.at[pl.ds(mid, block_rows)], target.at[16 : 16 + block_rows])
            copy_in(speed_ref.at[pl.ds(below, 16)], target.at[16 + block_rows :])
    speed_count = len(copies)
    for b in range(2):
        block = 2 * b + core
        start = first_row(block, src_ref.shape[2])
        landing = pl.ds(pl.multiple_of(start - block * CORE_ROWS + GUARD + TILE, TILE), ROWS)
        rows = pl.ds(start, ROWS)
        copy_in(src_ref.at[:, 0, rows, :], waves.at[2 * b, 0:2, landing, :])
        copy_in(rec_ref.at[:, 0, rows, :], waves.at[2 * b, 2:4, landing, :])
        copy_in(message_ref.at[4 * b : 4 * b + 4], waves.at[2 * b + 1, :, landing, :])
    for k in range(2):
        copy_in(halo_refs[k], sides.at[k])

    guard = jnp.zeros((TILE, LANES), F32)
    for buffer in (first, second):
        for part in range(4):
            buffer[part, 0:GUARD, :] = guard
            buffer[part, GUARD + ROWS :, :] = guard
    images[...] = jnp.zeros_like(images)

    for copy in copies[:speed_count]:
        copy.wait()
    tiles = ROWS // TILE
    dims = (tiles, TILE, LANES)
    lane = lax.broadcasted_iota(jnp.int32, dims, 2)
    place = lane & (WIN - 1)
    tile = lax.broadcasted_iota(jnp.int32, dims, 0)
    on_grid = jnp.logical_not(
        ((place < 4) & (strip == 0)) | ((place >= 28) & (strip == strips - 1))
    )
    upper = (((lane + 112) >> 6) & 1) == 1
    for depth in range(2):
        windows = []
        for b in range(2):
            block = 2 * b + core
            live = jnp.logical_not(
                ((tile == 0) & (block == 0)) | ((tile == tiles - 1) & (block == BLOCKS - 1))
            )
            here = jnp.stack(
                [stage[depth, b, 7 + SPAN * i : 15 + SPAN * i, :] for i in range(tiles)]
            )
            beside = jnp.stack(
                [
                    jnp.broadcast_to(
                        stage[depth, b, 15 + SPAN * i : 16 + SPAN * i, :], (TILE, LANES)
                    )
                    for i in range(tiles)
                ]
            )
            beside = pltpu.roll(beside, 0, 2, stride=16, stride_axis=1)
            window = jnp.where((lane >= 28) & (lane < 36), pltpu.roll(beside, 44, 2), 0.0)
            window = jnp.where((lane >= 4) & (lane < 16), pltpu.roll(here, 4, 2), window)
            window = jnp.where((lane >= 16) & (lane < 28), pltpu.roll(here, 28, 2), window)
            window = window + pltpu.roll(window, WIN, 2)
            window = window + pltpu.roll(window, 2 * WIN, 2)
            windows.append((window, jnp.where(live, window, 0.0)))
            speed[b, depth] = (phase_depth / here).reshape(ROWS, LANES)
            coef[b, depth] = jnp.where(live, fd_coef * here, 0.0).reshape(ROWS, LANES)
        window = jnp.where(upper, windows[1][0], windows[0][0])
        speed[2, depth] = (phase_depth / window).reshape(ROWS, LANES)
        window = jnp.where(upper, windows[1][1], windows[0][1])
        coef[2, depth] = jnp.where(on_grid, fd_coef * window, 0.0).reshape(ROWS, LANES)

    for copy in copies[speed_count:]:
        copy.wait()

    @pl.when(core == 0)
    def _():
        for m in range(2):
            for part in range(4):
                waves[m, part, GUARD : GUARD + TILE, :] = guard

    @pl.when(core == 1)
    def _():
        for m in range(2, 4):
            for part in range(4):
                waves[m, part, GUARD + ROWS - TILE : GUARD + ROWS, :] = guard

    def turned(k, low, high, shift):
        return pltpu.roll(sides[k, low:high, :], (WIN * (shift - core)) & (LANES - 1), 1)

    def pick(low, high, shift):
        odd = ((lanes_of(high - low) >> 5) & 1) == 1
        return jnp.where(odd, turned(1, low, high, shift + 1), turned(0, low, high, shift))

    tile_lane = lanes_of(TILE)
    above = pick(CORE_ROWS - TILE, CORE_ROWS, 1)
    above = jnp.where((tile_lane < 2 * WIN) & (core == 0), 0.0, above)
    below = pick(0, TILE, LANES // WIN - 1)
    below = jnp.where((tile_lane >= 2 * WIN) & (core == 1), 0.0, below)
    beside = jnp.concatenate([above, pick(0, CORE_ROWS, 0), below])
    lane = lanes_of(ROWS)
    place = lane & (WIN - 1)
    for part in range(4):
        own = waves[0, part, GUARD : GUARD + ROWS, :]
        for m in range(1, ITEMS):
            value = lane_roll(waves[m, part, GUARD : GUARD + ROWS, :], WIN * m)
            own = jnp.where((((lane + 16) >> 5) & 3) == m, value, own)
        window = lane_roll(beside, 28 - 8 * part)
        window = jnp.where((place >= 4) & (place < 16), lane_roll(own, 36), window)
        window = jnp.where((place >= 16) & (place < 28), lane_roll(own, 28), window)
        waves[ITEMS, part, GUARD : GUARD + ROWS, :] = window
    rows = [sides[k, CORE_ROWS : CORE_ROWS + TILE, :] for k in range(2)]
    odd = (((tile_lane + 112) >> 5) & 1) == 1
    for m in range(ITEMS):
        omega[m * TILE : (m + 1) * TILE, :] = rows[m & 1]
    omega[ITEMS * TILE :, :] = jnp.where(odd, rows[1], rows[0])

    chunks = ROWS // CHUNK

    def turn(values, depth, kind, row, freq_row):
        theta = freq_row * speed[kind, depth, pl.ds(row, CHUNK), :]
        sine, cosine = sin_cos(theta)
        src_re, src_im, rec_re, rec_im = values
        return (
            src_re * cosine - src_im * sine,
            src_re * sine + src_im * cosine,
            rec_re * cosine + rec_im * sine,
            rec_im * cosine - rec_re * sine,
        )

    def substep(buffer, depth, kind, row, freq_inverse):
        step = coef[kind, depth, pl.ds(row, CHUNK), :] * freq_inverse
        centers = []
        laps = []
        for part in range(4):
            center = buffer[part, pl.ds(row + GUARD, CHUNK), :]
            up = buffer[part, pl.ds(row + GUARD - 1, CHUNK), :]
            down = buffer[part, pl.ds(row + GUARD + 1, CHUNK), :]
            across = lane_roll(center, 1) + lane_roll(center, LANES - 1)
            centers.append(center)
            laps.append((across + (up + down)) - 4.0 * center)
        src_re, src_im, rec_re, rec_im = centers
        return (
            src_re - step * laps[1],
            src_im + step * laps[0],
            rec_re + step * laps[3],
            rec_im - step * laps[2],
        )

    def store(buffer, row, values):
        for part in range(4):
            buffer[part, pl.ds(row + GUARD, CHUNK), :] = values[part]

    def product(values):
        return values[0] * values[2] + values[1] * values[3]

    def add_image(kind, depth, row, value):
        low, high = max(row, TILE), min(row + CHUNK, TILE + CORE_ROWS)
        if low < high:
            images[kind, depth, low - TILE : high - TILE, :] += value[low - row : high - row, :]

    def item(k, carry):
        kind = k >> 1
        freq_row = omega[pl.ds(pl.multiple_of(k * TILE, TILE), 1), :]
        freq_inverse = 1.0 / freq_row

        for j in range(chunks):
            row = j * CHUNK
            values = [waves[k, part, pl.ds(row + GUARD, CHUNK), :] for part in range(4)]
            store(first, row, turn(values, 0, kind, row, freq_row))
        for j in range(chunks):
            store(second, j * CHUNK, substep(first, 0, kind, j * CHUNK, freq_inverse))
        for j in range(chunks):
            row = j * CHUNK
            values = substep(second, 0, kind, row, freq_inverse)
            add_image(kind, 0, row, product(values))
            store(first, row, turn(values, 1, kind, row, freq_row))
        for j in range(chunks):
            store(second, j * CHUNK, substep(first, 1, kind, j * CHUNK, freq_inverse))
        for j in range(chunks):
            values = substep(second, 1, kind, j * CHUNK, freq_inverse)
            add_image(kind, 1, j * CHUNK, product(values))
        return carry

    lax.fori_loop(0, ITEMS + 1, item, 0)
    lane = lanes_of(CORE_ROWS)
    mine = freq >> 1
    for depth in range(2):
        value = images[2, depth]
        value = value + lane_roll(value, -WIN)
        finished = []
        for b in range(2):
            image = jnp.where(lane < HALO, lane_roll(value, -64 * b - 36), images[b, depth])
            image = jnp.where(lane >= LANES - HALO, lane_roll(value, 100 - 64 * b), image)
            finished.append(image)
        own_ref[depth] = jnp.where(mine == 0, finished[0], finished[1])
        send_ref[depth] = jnp.where(mine == 0, finished[1], finished[0])


def shape(*dims):
    return jax.ShapeDtypeStruct(dims, F32)


def shards(source, receiver, velocity, omega):
    strips = lax.axis_size("strip")
    freqs = lax.axis_size("freq")
    vmem = pl.BlockSpec(memory_space=pltpu.VMEM)
    anywhere = pl.BlockSpec(memory_space=pl.ANY)

    def across(x, k):
        return lax.ppermute(x, "freq", [(i, i ^ k) for i in range(freqs)])

    packed = pl.pallas_call(
        pack_speed,
        out_shape=shape(SPAN * strips, LANES),
        in_specs=[anywhere],
        out_specs=vmem,
        scratch_shapes=[
            pltpu.VMEM((TILE, strips * LANES), F32),
            pltpu.SemaphoreType.DMA,
        ],
    )(velocity)
    speeds = lax.all_to_all(
        packed.reshape(strips, 1, SPAN * LANES), "strip", split_axis=0, concat_axis=0, tiled=True
    ).reshape(SPAN * strips, LANES)
    other_speeds = across(speeds, 1)

    edges, message = pl.pallas_call(
        cut_waves,
        out_shape=[shape(CORE_ROWS, LANES), shape(8, ROWS, LANES)],
        in_specs=[vmem, vmem],
        out_specs=[vmem, vmem],
    )(source, receiver)
    from_left = lax.ppermute(edges, "strip", [(i, i + 1) for i in range(strips - 1)])
    from_right = lax.ppermute(edges, "strip", [(i + 1, i) for i in range(strips - 1)])
    message = across(message, 1)
    first_half = (lanes_of(CORE_ROWS) & 7) < 4
    halos = jnp.concatenate(
        [
            jnp.where(first_half, from_right, from_left),
            jnp.broadcast_to(omega[:, None], (TILE, LANES)),
        ]
    )

    own, send = pl.pallas_call(
        march,
        out_shape=[shape(2, CORE_ROWS, LANES)] * 2,
        in_specs=[anywhere] * 7,
        out_specs=[vmem] * 2,
        scratch_shapes=[
            pltpu.VMEM((ITEMS + 1, 4, ROWS + 2 * GUARD, LANES), F32),
            pltpu.VMEM((2, CORE_ROWS + TILE, LANES), F32),
            pltpu.VMEM((2, 2, 32 + SPAN * CORE_ROWS // TILE, LANES), F32),
            pltpu.VMEM((3, 2, ROWS, LANES), F32),
            pltpu.VMEM((3, 2, ROWS, LANES), F32),
            pltpu.VMEM(((ITEMS + 1) * TILE, LANES), F32),
            pltpu.VMEM((4, ROWS + 2 * GUARD, LANES), F32),
            pltpu.VMEM((4, ROWS + 2 * GUARD, LANES), F32),
            pltpu.VMEM((3, 2, CORE_ROWS, LANES), F32),
            pltpu.SemaphoreType.DMA((20,)),
        ],
        compiler_params=pltpu.CompilerParams(vmem_limit_bytes=16 * 1024 * 1024),
    )(speeds, other_speeds, source, receiver, message, halos, across(halos, 1))
    return own + across(send, 2)


def solution(mesh):
    return jax.shard_map(
        shards,
        mesh=mesh,
        in_specs=(
            P(None, "freq", None, "strip"),
            P(None, "freq", None, "strip"),
            P(None, "strip", None),
            P("freq"),
        ),
        out_specs=P(None, "freq", "strip"),
        check_vma=False,
    )
```

```python
import functools

import jax
import jax.numpy as jnp
from jax import lax
from jax.experimental import pallas as pl
from jax.experimental.pallas import tpu as pltpu
from jax.sharding import PartitionSpec as P

BLOCKS = 4
ITEMS = 4
LANES = 128
TILE = 8
WIN = 32
HALO = 4
CORE_ROWS = 128
ROWS = CORE_ROWS + 2 * TILE
GUARD = TILE
CHUNK = 72
SPAN = 9
GROUPS = 4

phase_depth = 2.0
fd_coef = 0.03

F32 = jnp.float32


def lanes_of(rows):
    return lax.broadcasted_iota(jnp.int32, (rows, LANES), 1)


def lane_roll(x, shift):
    return pltpu.roll(x, shift % LANES, 1)


def pack_speed(vel_ref, out_ref, held, packed, sems):
    core = lax.axis_index("freq") & 1
    strips = vel_ref.shape[2] // LANES
    group = strips // GROUPS
    width = group * LANES
    reads = []
    for step in range(GROUPS):
        columns = slice(step * width, (step + 1) * width)
        reads.append(
            pltpu.make_async_copy(
                vel_ref.at[core, :, columns], held.at[:, columns], sems.at[0, step]
            )
        )
        reads[step].start()
    dims = (group, TILE, LANES)
    lane = lax.broadcasted_iota(jnp.int32, dims, 2)
    sublane = lax.broadcasted_iota(jnp.int32, dims, 1)

    def strip_of(strip):
        strip = min(max(strip, 0), strips - 1)
        return held[:, strip * LANES : (strip + 1) * LANES]

    writes = []
    reads[0].wait()
    for step in range(GROUPS):
        if step + 1 < GROUPS:
            reads[step + 1].wait()
        span = [strip_of(step * group + i) for i in range(-1, group + 1)]
        left = pltpu.roll(jnp.stack(span[:group]), 2 * HALO, 2)
        beside = jnp.where(lane < HALO, jnp.stack(span[2:]), left)
        beside = jnp.where(lane < 2 * HALO, beside, 0.0)
        for shift in (16, 32, 64):
            beside = beside + pltpu.roll(beside, shift, 2)
        beside = jnp.where((lane >> 4) == 7 - sublane, beside, 0.0)
        beside = jnp.sum(beside, axis=1, keepdims=True)
        rows = slice(step * group * SPAN, (step + 1) * group * SPAN)
        out = packed.at[rows]
        for i in range(group):
            out[SPAN * i : SPAN * i + TILE, :] = span[i + 1]
            out[SPAN * i + TILE : SPAN * (i + 1), :] = beside[i]
        writes.append(
            pltpu.make_async_copy(packed.at[rows], out_ref.at[rows], sems.at[1, step])
        )
        writes[step].start()
    for write in writes:
        write.wait()


def first_row(block, rows):
    start = jnp.clip(block * CORE_ROWS - TILE, 0, rows - ROWS)
    return pl.multiple_of(start, TILE)


def cut_waves(src_ref, rec_ref, edges_ref, message_ref):
    other = 1 - (lax.axis_index("freq") & 1)
    fields = (src_ref.at[0, 0], src_ref.at[1, 0], rec_ref.at[0, 0], rec_ref.at[1, 0])
    lane = lanes_of(CORE_ROWS)
    packed = jnp.zeros((CORE_ROWS, LANES), F32)
    for group in range(BLOCKS):
        for part, field in enumerate(fields):
            slot = 4 * group + part
            value = field[group * CORE_ROWS : (group + 1) * CORE_ROWS, :]
            packed = jnp.where((lane >> 3) == slot, lane_roll(value, 8 * slot + 4), packed)
    edges_ref[...] = jnp.where((lane & 7) < 4, lane_roll(packed, -4), lane_roll(packed, 4))
    for b in range(2):
        rows = pl.ds(first_row(2 * b + other, src_ref.shape[2]), ROWS)
        for part, field in enumerate(fields):
            message_ref[4 * b + part] = field[rows, :]


SIN_TERMS = (1.0, -0.166666641831398, 0.008333218283951283, -0.00019823516777250916, 2.643730113049969e-06)
COS_TERMS = (1.0, -0.5, 0.041666656732559204, -0.0013888673856854439, 2.4778757506283e-05, -2.6437069777784927e-07)


def horner(terms, x):
    value = terms[-1]
    for term in terms[-2::-1]:
        value = value * x + term
    return value


def sin_cos(x):
    t = 0.5 * x - 0.7853981633974483
    square = t * t
    sine = t * horner(SIN_TERMS, square)
    cosine = horner(COS_TERMS, square)
    twice = -2.0 * sine
    return 1.0 + twice * sine, twice * cosine


def march(*refs):
    speed_refs, src_ref, rec_ref, message_ref, halo_refs = refs[:2], *refs[2:5], refs[5:7]
    own_ref, send_ref = refs[7:9]
    waves, sides, stage, speed, coef, omega, first, second, images, sems = refs[9:]
    freq = lax.axis_index("freq")
    core = freq & 1
    strip = lax.axis_index("strip")
    strips = lax.axis_size("strip")
    copies = []

    def copy_in(source, target):
        copy = pltpu.make_async_copy(source, target, sems.at[len(copies)])
        copy.start()
        copies.append(copy)

    block_rows = SPAN * (CORE_ROWS // TILE)
    for b in range(2):
        mid = pl.multiple_of((2 * b + core) * block_rows, TILE)
        above = pl.multiple_of(jnp.maximum(mid - 16, 0), TILE)
        below = pl.multiple_of(jnp.minimum(mid + block_rows, strips * SPAN - 16), TILE)
        for which, speed_ref in enumerate(speed_refs):
            target = stage.at[core ^ which, b]
            copy_in(speed_ref.at[pl.ds(above, 16)], target.at[0:16])
            copy_in(speed_ref.at[pl.ds(mid, block_rows)], target.at[16 : 16 + block_rows])
            copy_in(speed_ref.at[pl.ds(below, 16)], target.at[16 + block_rows :])
    speed_count = len(copies)
    for b in range(2):
        block = 2 * b + core
        start = first_row(block, src_ref.shape[2])
        landing = pl.ds(pl.multiple_of(start - block * CORE_ROWS + GUARD + TILE, TILE), ROWS)
        rows = pl.ds(start, ROWS)
        copy_in(src_ref.at[:, 0, rows, :], waves.at[2 * b, 0:2, landing, :])
        copy_in(rec_ref.at[:, 0, rows, :], waves.at[2 * b, 2:4, landing, :])
        copy_in(message_ref.at[4 * b : 4 * b + 4], waves.at[2 * b + 1, :, landing, :])
    for k in range(2):
        copy_in(halo_refs[k], sides.at[k])

    guard = jnp.zeros((TILE, LANES), F32)
    for buffer in (first, second):
        for part in range(4):
            buffer[part, 0:GUARD, :] = guard
            buffer[part, GUARD + ROWS :, :] = guard
    images[...] = jnp.zeros_like(images)

    for copy in copies[:speed_count]:
        copy.wait()
    tiles = ROWS // TILE
    dims = (tiles, TILE, LANES)
    lane = lax.broadcasted_iota(jnp.int32, dims, 2)
    place = lane & (WIN - 1)
    tile = lax.broadcasted_iota(jnp.int32, dims, 0)
    on_grid = jnp.logical_not(
        ((place < 4) & (strip == 0)) | ((place >= 28) & (strip == strips - 1))
    )
    for depth in range(2):
        window = jnp.zeros(dims, F32)
        window_live = place < 0
        for b in range(2):
            block = 2 * b + core
            live = jnp.logical_not(
                ((tile == 0) & (block == 0)) | ((tile == tiles - 1) & (block == BLOCKS - 1))
            )
            here = jnp.stack(
                [stage[depth, b, 7 + SPAN * i : 15 + SPAN * i, :] for i in range(tiles)]
            )
            beside = jnp.stack(
                [
                    jnp.broadcast_to(
                        stage[depth, b, 15 + SPAN * i : 16 + SPAN * i, :], (TILE, LANES)
                    )
                    for i in range(tiles)
                ]
            )
            beside = pltpu.roll(beside, 0, 2, stride=16, stride_axis=1)
            base = 64 * b

            def lanes_in(low, high):
                return (lane >= base + low) & (lane < base + high)

            window = jnp.where(
                lanes_in(16, 28), pltpu.roll(here, (base + 28) % LANES, 2), window
            )
            window = jnp.where(
                lanes_in(28, 36), pltpu.roll(beside, (base + 44) % LANES, 2), window
            )
            window = jnp.where(
                lanes_in(36, 48), pltpu.roll(here, (base + 36) % LANES, 2), window
            )
            window_live = window_live | (live & ((((lane + 112) >> 6) & 1) == b))
            speed[b, depth] = (phase_depth / here).reshape(ROWS, LANES)
            coef[b, depth] = jnp.where(live, fd_coef * here, 0.0).reshape(ROWS, LANES)
        window = window + pltpu.roll(window, WIN, 2)
        speed[2, depth] = (phase_depth / window).reshape(ROWS, LANES)
        coef[2, depth] = jnp.where(
            on_grid & window_live, fd_coef * window, 0.0
        ).reshape(ROWS, LANES)

    for copy in copies[speed_count:]:
        copy.wait()

    @pl.when(core == 0)
    def _():
        for m in range(2):
            for part in range(4):
                waves[m, part, GUARD : GUARD + TILE, :] = guard

    @pl.when(core == 1)
    def _():
        for m in range(2, 4):
            for part in range(4):
                waves[m, part, GUARD + ROWS - TILE : GUARD + ROWS, :] = guard

    def turned(k, low, high, shift):
        return pltpu.roll(sides[k, low:high, :], (WIN * (shift - core)) & (LANES - 1), 1)

    def pick(low, high, shift):
        odd = ((lanes_of(high - low) >> 5) & 1) == 1
        return jnp.where(odd, turned(1, low, high, shift + 1), turned(0, low, high, shift))

    tile_lane = lanes_of(TILE)
    above = pick(CORE_ROWS - TILE, CORE_ROWS, 1)
    above = jnp.where((tile_lane < 2 * WIN) & (core == 0), 0.0, above)
    below = pick(0, TILE, LANES // WIN - 1)
    below = jnp.where((tile_lane >= 2 * WIN) & (core == 1), 0.0, below)
    beside = jnp.concatenate([above, pick(0, CORE_ROWS, 0), below])
    lane = lanes_of(ROWS)
    place = lane & (WIN - 1)
    for part in range(4):
        own = waves[0, part, GUARD : GUARD + ROWS, :]
        for m in range(1, ITEMS):
            value = lane_roll(waves[m, part, GUARD : GUARD + ROWS, :], WIN * m)
            own = jnp.where((((lane + 16) >> 5) & 3) == m, value, own)
        window = lane_roll(beside, 28 - 8 * part)
        window = jnp.where((place >= 4) & (place < 16), lane_roll(own, 36), window)
        window = jnp.where((place >= 16) & (place < 28), lane_roll(own, 28), window)
        waves[ITEMS, part, GUARD : GUARD + ROWS, :] = window
    rows = [sides[k, CORE_ROWS : CORE_ROWS + TILE, :] for k in range(2)]
    odd = (((tile_lane + 112) >> 5) & 1) == 1
    for m in range(ITEMS):
        omega[m * TILE : (m + 1) * TILE, :] = rows[m & 1]
    omega[ITEMS * TILE :, :] = jnp.where(odd, rows[1], rows[0])

    chunks = ROWS // CHUNK

    def turn(values, depth, kind, row, freq_row):
        theta = freq_row * speed[kind, depth, pl.ds(row, CHUNK), :]
        sine, cosine = sin_cos(theta)
        src_re, src_im, rec_re, rec_im = values
        return (
            src_re * cosine - src_im * sine,
            src_re * sine + src_im * cosine,
            rec_re * cosine + rec_im * sine,
            rec_im * cosine - rec_re * sine,
        )

    def substep(buffer, depth, kind, row, freq_inverse):
        step = coef[kind, depth, pl.ds(row, CHUNK), :] * freq_inverse
        centers = []
        laps = []
        for part in range(4):
            center = buffer[part, pl.ds(row + GUARD, CHUNK), :]
            up = buffer[part, pl.ds(row + GUARD - 1, CHUNK), :]
            down = buffer[part, pl.ds(row + GUARD + 1, CHUNK), :]
            across = lane_roll(center, 1) + lane_roll(center, LANES - 1)
            centers.append(center)
            laps.append((across + (up + down)) - 4.0 * center)
        src_re, src_im, rec_re, rec_im = centers
        return (
            src_re - step * laps[1],
            src_im + step * laps[0],
            rec_re + step * laps[3],
            rec_im - step * laps[2],
        )

    def store(buffer, row, values):
        for part in range(4):
            buffer[part, pl.ds(row + GUARD, CHUNK), :] = values[part]

    def product(values):
        return values[0] * values[2] + values[1] * values[3]

    def add_image(kind, depth, row, value):
        low, high = max(row, TILE), min(row + CHUNK, TILE + CORE_ROWS)
        if low < high:
            images[kind, depth, low - TILE : high - TILE, :] += value[low - row : high - row, :]

    def item(k, carry):
        kind = k >> 1
        freq_row = omega[pl.ds(pl.multiple_of(k * TILE, TILE), 1), :]
        freq_inverse = 1.0 / freq_row

        for j in range(chunks):
            row = j * CHUNK
            values = [waves[k, part, pl.ds(row + GUARD, CHUNK), :] for part in range(4)]
            store(first, row, turn(values, 0, kind, row, freq_row))
        for j in range(chunks):
            store(second, j * CHUNK, substep(first, 0, kind, j * CHUNK, freq_inverse))
        for j in range(chunks):
            row = j * CHUNK
            values = substep(second, 0, kind, row, freq_inverse)
            add_image(kind, 0, row, product(values))
            store(first, row, turn(values, 1, kind, row, freq_row))
        for j in range(chunks):
            store(second, j * CHUNK, substep(first, 1, kind, j * CHUNK, freq_inverse))
        for j in range(chunks):
            values = substep(second, 1, kind, j * CHUNK, freq_inverse)
            add_image(kind, 1, j * CHUNK, product(values))
        return carry

    lax.fori_loop(0, ITEMS + 1, item, 0)
    lane = lanes_of(CORE_ROWS)
    mine = freq >> 1
    for depth in range(2):
        value = images[2, depth]
        value = value + lane_roll(value, -WIN)
        finished = []
        for b in range(2):
            image = jnp.where(lane < HALO, lane_roll(value, -64 * b - 36), images[b, depth])
            image = jnp.where(lane >= LANES - HALO, lane_roll(value, 100 - 64 * b), image)
            finished.append(image)
        own_ref[depth] = jnp.where(mine == 0, finished[0], finished[1])
        send_ref[depth] = jnp.where(mine == 0, finished[1], finished[0])


def shape(*dims):
    return jax.ShapeDtypeStruct(dims, F32)


def shards(source, receiver, velocity, omega):
    strips = lax.axis_size("strip")
    freqs = lax.axis_size("freq")
    vmem = pl.BlockSpec(memory_space=pltpu.VMEM)
    anywhere = pl.BlockSpec(memory_space=pl.ANY)

    def across(x, k):
        return lax.ppermute(x, "freq", [(i, i ^ k) for i in range(freqs)])

    packed = pl.pallas_call(
        pack_speed,
        out_shape=shape(SPAN * strips, LANES),
        in_specs=[anywhere],
        out_specs=anywhere,
        scratch_shapes=[
            pltpu.VMEM((TILE, strips * LANES), F32),
            pltpu.VMEM((SPAN * strips, LANES), F32),
            pltpu.SemaphoreType.DMA((2, GROUPS)),
        ],
    )(velocity)
    speeds = lax.all_to_all(
        packed.reshape(strips, 1, SPAN * LANES), "strip", split_axis=0, concat_axis=0, tiled=True
    ).reshape(SPAN * strips, LANES)
    other_speeds = across(speeds, 1)

    edges, message = pl.pallas_call(
        cut_waves,
        out_shape=[shape(CORE_ROWS, LANES), shape(8, ROWS, LANES)],
        in_specs=[vmem, vmem],
        out_specs=[vmem, vmem],
    )(source, receiver)
    def swap(x, pairs):
        return lax.ppermute(x, "strip", [p for i, j in pairs for p in ((i, j), (j, i))])

    with_far = swap(edges, [(i, i + 1) for i in range(1, strips - 1, 2)])
    with_near = swap(edges, [(i, i + 1) for i in range(0, strips, 2)])
    message = across(message, 1)
    parity = lax.axis_index("strip") & 1
    from_near = (((lanes_of(CORE_ROWS) >> 2) ^ parity) & 1) == 0
    halos = jnp.concatenate(
        [
            jnp.where(from_near, with_near, with_far),
            jnp.broadcast_to(omega[:, None], (TILE, LANES)),
        ]
    )

    own, send = pl.pallas_call(
        march,
        out_shape=[shape(2, CORE_ROWS, LANES)] * 2,
        in_specs=[anywhere] * 7,
        out_specs=[vmem] * 2,
        scratch_shapes=[
            pltpu.VMEM((ITEMS + 1, 4, ROWS + 2 * GUARD, LANES), F32),
            pltpu.VMEM((2, CORE_ROWS + TILE, LANES), F32),
            pltpu.VMEM((2, 2, 32 + SPAN * CORE_ROWS // TILE, LANES), F32),
            pltpu.VMEM((3, 2, ROWS, LANES), F32),
            pltpu.VMEM((3, 2, ROWS, LANES), F32),
            pltpu.VMEM(((ITEMS + 1) * TILE, LANES), F32),
            pltpu.VMEM((4, ROWS + 2 * GUARD, LANES), F32),
            pltpu.VMEM((4, ROWS + 2 * GUARD, LANES), F32),
            pltpu.VMEM((3, 2, CORE_ROWS, LANES), F32),
            pltpu.SemaphoreType.DMA((20,)),
        ],
        compiler_params=pltpu.CompilerParams(vmem_limit_bytes=16 * 1024 * 1024),
    )(speeds, other_speeds, source, receiver, message, halos, across(halos, 1))
    return own + across(send, 2)


def solution(mesh):
    return jax.shard_map(
        shards,
        mesh=mesh,
        in_specs=(
            P(None, "freq", None, "strip"),
            P(None, "freq", None, "strip"),
            P(None, "strip", None),
            P("freq"),
        ),
        out_specs=P(None, "freq", "strip"),
        check_vma=False,
    )
```

```python
import functools

import jax
import jax.numpy as jnp
from jax import lax
from jax.experimental import pallas as pl
from jax.experimental.pallas import tpu as pltpu
from jax.sharding import PartitionSpec as P

BLOCKS = 4
ITEMS = 4
LANES = 128
TILE = 8
WIN = 32
HALO = 4
CORE_ROWS = 128
ROWS = CORE_ROWS + 2 * TILE
GUARD = TILE
CHUNK = 72
SPAN = 9
GROUPS = 2

phase_depth = 2.0
fd_coef = 0.03

F32 = jnp.float32


def lanes_of(rows):
    return lax.broadcasted_iota(jnp.int32, (rows, LANES), 1)


def lane_roll(x, shift):
    return pltpu.roll(x, shift % LANES, 1)


def pack_speed(vel_ref, out_ref, held, packed, sems):
    core = lax.axis_index("freq") & 1
    strips = vel_ref.shape[2] // LANES
    group = strips // GROUPS
    width = group * LANES
    reads = []
    for step in range(GROUPS):
        columns = slice(step * width, (step + 1) * width)
        reads.append(
            pltpu.make_async_copy(
                vel_ref.at[core, :, columns], held.at[:, columns], sems.at[0, step]
            )
        )
        reads[step].start()
    dims = (group, TILE, LANES)
    lane = lax.broadcasted_iota(jnp.int32, dims, 2)
    sublane = lax.broadcasted_iota(jnp.int32, dims, 1)

    def strip_of(strip):
        strip = min(max(strip, 0), strips - 1)
        return held[:, strip * LANES : (strip + 1) * LANES]

    writes = []
    reads[0].wait()
    for step in range(GROUPS):
        if step + 1 < GROUPS:
            reads[step + 1].wait()
        span = [strip_of(step * group + i) for i in range(-1, group + 1)]
        left = pltpu.roll(jnp.stack(span[:group]), 2 * HALO, 2)
        beside = jnp.where(lane < HALO, jnp.stack(span[2:]), left)
        beside = jnp.where(lane < 2 * HALO, beside, 0.0)
        for shift in (16, 32, 64):
            beside = beside + pltpu.roll(beside, shift, 2)
        beside = jnp.where((lane >> 4) == 7 - sublane, beside, 0.0)
        beside = jnp.sum(beside, axis=1, keepdims=True)
        rows = slice(step * group * SPAN, (step + 1) * group * SPAN)
        out = packed.at[rows]
        for i in range(group):
            out[SPAN * i : SPAN * i + TILE, :] = span[i + 1]
            out[SPAN * i + TILE : SPAN * (i + 1), :] = beside[i]
        writes.append(
            pltpu.make_async_copy(packed.at[rows], out_ref.at[rows], sems.at[1, step])
        )
        writes[step].start()
    for write in writes:
        write.wait()


def first_row(block, rows):
    start = jnp.clip(block * CORE_ROWS - TILE, 0, rows - ROWS)
    return pl.multiple_of(start, TILE)


def cut_waves(src_any, rec_any, edges_ref, message_ref, src_ref, rec_ref, sems):
    copies, copy_in = copier(sems)
    copy_in(src_any, src_ref)
    copy_in(rec_any, rec_ref)
    other = 1 - (lax.axis_index("freq") & 1)
    for copy in copies:
        copy.wait()
    fields = (src_ref.at[0, 0], src_ref.at[1, 0], rec_ref.at[0, 0], rec_ref.at[1, 0])
    lane = lanes_of(CORE_ROWS)
    packed = jnp.zeros((CORE_ROWS, LANES), F32)
    for group in range(BLOCKS):
        for part, field in enumerate(fields):
            slot = 4 * group + part
            value = field[group * CORE_ROWS : (group + 1) * CORE_ROWS, :]
            packed = jnp.where((lane >> 3) == slot, lane_roll(value, 8 * slot + 4), packed)
    edges_ref[...] = jnp.where((lane & 7) < 4, lane_roll(packed, -4), lane_roll(packed, 4))
    for b in range(2):
        rows = pl.ds(first_row(2 * b + other, src_ref.shape[2]), ROWS)
        for part, field in enumerate(fields):
            message_ref[4 * b + part] = field[rows, :]


SIN_TERMS = (1.0, -0.166666641831398, 0.008333218283951283, -0.00019823516777250916, 2.643730113049969e-06)
COS_TERMS = (1.0, -0.5, 0.041666656732559204, -0.0013888673856854439, 2.4778757506283e-05, -2.6437069777784927e-07)


def horner(terms, x):
    value = terms[-1]
    for term in terms[-2::-1]:
        value = value * x + term
    return value


def sin_cos(x):
    t = 0.5 * x - 0.7853981633974483
    square = t * t
    sine = t * horner(SIN_TERMS, square)
    cosine = horner(COS_TERMS, square)
    twice = -2.0 * sine
    return 1.0 + twice * sine, twice * cosine


def stepper(waves, speed, coef, omega, first, second, images):
    chunks = ROWS // CHUNK
    guard = jnp.zeros((TILE, LANES), F32)
    for buffer in (first, second):
        for part in range(4):
            buffer[part, 0:GUARD, :] = guard
            buffer[part, GUARD + ROWS :, :] = guard
    images[...] = jnp.zeros_like(images)

    def turn(values, depth, kind, row, freq_row):
        theta = freq_row * speed[kind, depth, pl.ds(row, CHUNK), :]
        sine, cosine = sin_cos(theta)
        src_re, src_im, rec_re, rec_im = values
        return (
            src_re * cosine - src_im * sine,
            src_re * sine + src_im * cosine,
            rec_re * cosine + rec_im * sine,
            rec_im * cosine - rec_re * sine,
        )

    def substep(buffer, depth, kind, row, freq_inverse):
        step = coef[kind, depth, pl.ds(row, CHUNK), :] * freq_inverse
        centers = []
        laps = []
        for part in range(4):
            center = buffer[part, pl.ds(row + GUARD, CHUNK), :]
            up = buffer[part, pl.ds(row + GUARD - 1, CHUNK), :]
            down = buffer[part, pl.ds(row + GUARD + 1, CHUNK), :]
            across = lane_roll(center, 1) + lane_roll(center, LANES - 1)
            centers.append(center)
            laps.append((across + (up + down)) - 4.0 * center)
        src_re, src_im, rec_re, rec_im = centers
        return (
            src_re - step * laps[1],
            src_im + step * laps[0],
            rec_re + step * laps[3],
            rec_im - step * laps[2],
        )

    def store(buffer, row, values):
        for part in range(4):
            buffer[part, pl.ds(row + GUARD, CHUNK), :] = values[part]

    def product(values):
        return values[0] * values[2] + values[1] * values[3]

    def add_image(kind, depth, row, value):
        low, high = max(row, TILE), min(row + CHUNK, TILE + CORE_ROWS)
        if low < high:
            images[kind, depth, low - TILE : high - TILE, :] += value[low - row : high - row, :]

    def item(k, kind):
        freq_row = omega[pl.ds(pl.multiple_of(k * TILE, TILE), 1), :]
        freq_inverse = 1.0 / freq_row

        for j in range(chunks):
            row = j * CHUNK
            values = [waves[k, part, pl.ds(row + GUARD, CHUNK), :] for part in range(4)]
            store(first, row, turn(values, 0, kind, row, freq_row))
        for j in range(chunks):
            store(second, j * CHUNK, substep(first, 0, kind, j * CHUNK, freq_inverse))
        for j in range(chunks):
            row = j * CHUNK
            values = substep(second, 0, kind, row, freq_inverse)
            add_image(kind, 0, row, product(values))
            store(first, row, turn(values, 1, kind, row, freq_row))
        for j in range(chunks):
            store(second, j * CHUNK, substep(first, 1, kind, j * CHUNK, freq_inverse))
        for j in range(chunks):
            values = substep(second, 1, kind, j * CHUNK, freq_inverse)
            add_image(kind, 1, j * CHUNK, product(values))

    return item


def clear_above(waves, items):
    for m in items:
        for part in range(4):
            waves[m, part, GUARD : GUARD + TILE, :] = jnp.zeros((TILE, LANES), F32)


def clear_below(waves, items):
    for m in items:
        for part in range(4):
            rows = slice(GUARD + ROWS - TILE, GUARD + ROWS)
            waves[m, part, rows, :] = jnp.zeros((TILE, LANES), F32)


def copier(sems):
    copies = []

    def copy_in(source, target):
        copy = pltpu.make_async_copy(source, target, sems.at[len(copies)])
        copy.start()
        copies.append(copy)

    return copies, copy_in


def copy_speeds(copy_in, speed_refs, stage, block, core):
    block_rows = SPAN * (CORE_ROWS // TILE)
    mid = pl.multiple_of(block * block_rows, TILE)
    above = pl.multiple_of(jnp.maximum(mid - 16, 0), TILE)
    below = pl.multiple_of(jnp.minimum(mid + block_rows, speed_refs[0].shape[0] - 16), TILE)
    for which, speed_ref in enumerate(speed_refs):
        target = stage.at[core ^ which]
        copy_in(speed_ref.at[pl.ds(above, 16)], target.at[0:16])
        copy_in(speed_ref.at[pl.ds(mid, block_rows)], target.at[16 : 16 + block_rows])
        copy_in(speed_ref.at[pl.ds(below, 16)], target.at[16 + block_rows :])


def copy_waves(copy_in, src_ref, rec_ref, message_ref, waves, block, b, m):
    start = first_row(block, src_ref.shape[2])
    landing = pl.ds(pl.multiple_of(start - block * CORE_ROWS + GUARD + TILE, TILE), ROWS)
    rows = pl.ds(start, ROWS)
    copy_in(src_ref.at[:, 0, rows, :], waves.at[m, 0:2, landing, :])
    copy_in(rec_ref.at[:, 0, rows, :], waves.at[m, 2:4, landing, :])
    copy_in(message_ref.at[pl.ds(4 * b, 4)], waves.at[m + 1, :, landing, :])


def tile_speeds(stage, depth):
    tiles = ROWS // TILE
    return jnp.stack([stage[depth, 7 + SPAN * i : 15 + SPAN * i, :] for i in range(tiles)])


def patch(image, value, b):
    lane = lanes_of(CORE_ROWS)
    image = jnp.where(lane < HALO, pltpu.roll(value, (2 * LANES - 64 * b - 36) & 127, 1), image)
    return jnp.where(
        lane >= LANES - HALO, pltpu.roll(value, (LANES + 100 - 64 * b) & 127, 1), image
    )


def march_sent(*refs):
    speed_refs, src_ref, rec_ref, message_ref, halo_refs = refs[:2], *refs[2:5], refs[5:7]
    send_ref, sums_ref = refs[7:9]
    waves, sides, stage, speed, coef, omega, first, second, images, sems = refs[9:]
    freq = lax.axis_index("freq")
    core = freq & 1
    strip = lax.axis_index("strip")
    strips = lax.axis_size("strip")
    copies, copy_in = copier(sems)
    for b in range(2):
        copy_speeds(copy_in, speed_refs, stage.at[b], 2 * b + core, core)
    speed_count = len(copies)
    for b in range(2):
        copy_waves(copy_in, src_ref, rec_ref, message_ref, waves, 2 * b + core, b, 2 * b)
    for k in range(2):
        copy_in(halo_refs[k], sides.at[k])

    item = stepper(waves, speed, coef, omega, first, second, images)
    for copy in copies[:speed_count]:
        copy.wait()
    tiles = ROWS // TILE
    dims = (tiles, TILE, LANES)
    lane = lax.broadcasted_iota(jnp.int32, dims, 2)
    place = lane & (WIN - 1)
    tile = lax.broadcasted_iota(jnp.int32, dims, 0)
    on_grid = jnp.logical_not(
        ((place < 4) & (strip == 0)) | ((place >= 28) & (strip == strips - 1))
    )
    for depth in range(2):
        window = jnp.zeros(dims, F32)
        window_live = place < 0
        for b in range(2):
            block = 2 * b + core
            live = jnp.logical_not(
                ((tile == 0) & (block == 0)) | ((tile == tiles - 1) & (block == BLOCKS - 1))
            )
            here = tile_speeds(stage.at[b], depth)
            beside = jnp.stack(
                [
                    jnp.broadcast_to(
                        stage[b, depth, 15 + SPAN * i : 16 + SPAN * i, :], (TILE, LANES)
                    )
                    for i in range(tiles)
                ]
            )
            beside = pltpu.roll(beside, 0, 2, stride=16, stride_axis=1)
            base = 64 * b

            def lanes_in(low, high):
                return (lane >= base + low) & (lane < base + high)

            window = jnp.where(
                lanes_in(16, 28), pltpu.roll(here, (base + 28) % LANES, 2), window
            )
            window = jnp.where(
                lanes_in(28, 36), pltpu.roll(beside, (base + 44) % LANES, 2), window
            )
            window = jnp.where(
                lanes_in(36, 48), pltpu.roll(here, (base + 36) % LANES, 2), window
            )
            window_live = window_live | (live & ((((lane + 112) >> 6) & 1) == b))
            speed[b, depth] = (phase_depth / here).reshape(ROWS, LANES)
            coef[b, depth] = jnp.where(live, fd_coef * here, 0.0).reshape(ROWS, LANES)
        window = window + pltpu.roll(window, WIN, 2)
        speed[2, depth] = (phase_depth / window).reshape(ROWS, LANES)
        coef[2, depth] = jnp.where(
            on_grid & window_live, fd_coef * window, 0.0
        ).reshape(ROWS, LANES)

    for copy in copies[speed_count:]:
        copy.wait()

    @pl.when(core == 0)
    def _():
        clear_above(waves, range(2))

    @pl.when(core == 1)
    def _():
        clear_below(waves, range(2, 4))

    def turned(k, low, high, shift):
        return pltpu.roll(sides[k, low:high, :], (WIN * (shift - core)) & (LANES - 1), 1)

    def pick(low, high, shift):
        odd = ((lanes_of(high - low) >> 5) & 1) == 1
        return jnp.where(odd, turned(1, low, high, shift + 1), turned(0, low, high, shift))

    tile_lane = lanes_of(TILE)
    above = pick(CORE_ROWS - TILE, CORE_ROWS, 1)
    above = jnp.where((tile_lane < 2 * WIN) & (core == 0), 0.0, above)
    below = pick(0, TILE, LANES // WIN - 1)
    below = jnp.where((tile_lane >= 2 * WIN) & (core == 1), 0.0, below)
    beside = jnp.concatenate([above, pick(0, CORE_ROWS, 0), below])
    lane = lanes_of(ROWS)
    place = lane & (WIN - 1)
    for part in range(4):
        own = waves[0, part, GUARD : GUARD + ROWS, :]
        for m in range(1, ITEMS):
            value = lane_roll(waves[m, part, GUARD : GUARD + ROWS, :], WIN * m)
            own = jnp.where((((lane + 16) >> 5) & 3) == m, value, own)
        window = lane_roll(beside, 28 - 8 * part)
        window = jnp.where((place >= 4) & (place < 16), lane_roll(own, 36), window)
        window = jnp.where((place >= 16) & (place < 28), lane_roll(own, 28), window)
        waves[ITEMS, part, GUARD : GUARD + ROWS, :] = window
    rows = [sides[k, CORE_ROWS : CORE_ROWS + TILE, :] for k in range(2)]
    odd = (((tile_lane + 112) >> 5) & 1) == 1
    for m in range(ITEMS):
        omega[m * TILE : (m + 1) * TILE, :] = rows[m & 1]
    omega[ITEMS * TILE :, :] = jnp.where(odd, rows[1], rows[0])

    sent = 1 - (freq >> 1)

    def step(j, carry):
        k = jnp.where(j == 2, ITEMS, 2 * sent + j)
        item(k, k >> 1)
        return carry

    lax.fori_loop(0, 3, step, 0)
    for depth in range(2):
        value = images[2, depth]
        value = value + lane_roll(value, -WIN)
        sums_ref[depth] = value
        send_ref[depth] = patch(images[sent, depth], value, sent)


def march_kept(*refs):
    speed_refs, src_ref, rec_ref, message_ref, halo_refs = refs[:2], *refs[2:5], refs[5:7]
    sums_ref, image_ref = refs[7:9]
    waves, stage, speed, coef, omega, first, second, images, sems = refs[9:]
    freq = lax.axis_index("freq")
    core = freq & 1
    b = freq >> 1
    copies, copy_in = copier(sems)
    copy_speeds(copy_in, speed_refs, stage, freq, core)
    copy_waves(copy_in, src_ref, rec_ref, message_ref, waves, freq, b, 0)
    for k in range(2):
        copy_in(
            halo_refs[k].at[CORE_ROWS : CORE_ROWS + TILE], omega.at[k * TILE : (k + 1) * TILE]
        )
    item = stepper(waves, speed, coef, omega, first, second, images)
    for copy in copies:
        copy.wait()
    tiles = ROWS // TILE
    tile = lax.broadcasted_iota(jnp.int32, (tiles, TILE, LANES), 0)
    live = jnp.logical_not(
        ((tile == 0) & (freq == 0)) | ((tile == tiles - 1) & (freq == BLOCKS - 1))
    )
    for depth in range(2):
        here = tile_speeds(stage, depth)
        speed[0, depth] = (phase_depth / here).reshape(ROWS, LANES)
        coef[0, depth] = jnp.where(live, fd_coef * here, 0.0).reshape(ROWS, LANES)

    @pl.when(freq == 0)
    def _():
        clear_above(waves, range(2))

    @pl.when(freq == BLOCKS - 1)
    def _():
        clear_below(waves, range(2))

    def step(k, carry):
        item(k, 0)
        return carry

    lax.fori_loop(0, 2, step, 0)
    for depth in range(2):
        image_ref[depth] = patch(images[0, depth], sums_ref[depth], b)


SMALL = pltpu.CompilerParams(vmem_limit_bytes=16 * 1024 * 1024)


def shape(*dims):
    return jax.ShapeDtypeStruct(dims, F32)


def shards(source, receiver, velocity, omega):
    strips = lax.axis_size("strip")
    freqs = lax.axis_size("freq")
    vmem = pl.BlockSpec(memory_space=pltpu.VMEM)
    anywhere = pl.BlockSpec(memory_space=pl.ANY)

    def across(x, k):
        return lax.ppermute(x, "freq", [(i, i ^ k) for i in range(freqs)])

    packed = pl.pallas_call(
        pack_speed,
        out_shape=shape(SPAN * strips, LANES),
        in_specs=[anywhere],
        out_specs=anywhere,
        scratch_shapes=[
            pltpu.VMEM((TILE, strips * LANES), F32),
            pltpu.VMEM((SPAN * strips, LANES), F32),
            pltpu.SemaphoreType.DMA((2, GROUPS)),
        ],
    )(velocity)
    speeds = lax.all_to_all(
        packed.reshape(strips, 1, SPAN * LANES), "strip", split_axis=0, concat_axis=0, tiled=True
    ).reshape(SPAN * strips, LANES)
    other_speeds = across(speeds, 1)

    edges, message = pl.pallas_call(
        cut_waves,
        out_shape=[shape(CORE_ROWS, LANES), shape(8, ROWS, LANES)],
        in_specs=[anywhere, anywhere],
        out_specs=[vmem, vmem],
        scratch_shapes=[pltpu.VMEM(source.shape, F32)] * 2 + [pltpu.SemaphoreType.DMA((2,))],
        compiler_params=SMALL,
    )(source, receiver)
    def swap(x, pairs):
        return lax.ppermute(x, "strip", [p for i, j in pairs for p in ((i, j), (j, i))])

    with_far = swap(edges, [(i, i + 1) for i in range(1, strips - 1, 2)])
    with_near = swap(edges, [(i, i + 1) for i in range(0, strips, 2)])
    message = across(message, 1)
    parity = lax.axis_index("strip") & 1
    from_near = (((lanes_of(CORE_ROWS) >> 2) ^ parity) & 1) == 0
    halos = jnp.concatenate(
        [
            jnp.where(from_near, with_near, with_far),
            jnp.broadcast_to(omega[:, None], (TILE, LANES)),
        ]
    )

    inputs = (speeds, other_speeds, source, receiver, message, halos, across(halos, 1))

    def scratch(items, kinds):
        return [
            pltpu.VMEM((kinds, 2, ROWS, LANES), F32),
            pltpu.VMEM((kinds, 2, ROWS, LANES), F32),
            pltpu.VMEM((items * TILE, LANES), F32),
            pltpu.VMEM((4, ROWS + 2 * GUARD, LANES), F32),
            pltpu.VMEM((4, ROWS + 2 * GUARD, LANES), F32),
            pltpu.VMEM((kinds, 2, CORE_ROWS, LANES), F32),
            pltpu.SemaphoreType.DMA((20,)),
        ]

    stage_rows = 32 + SPAN * CORE_ROWS // TILE
    send, sums = pl.pallas_call(
        march_sent,
        out_shape=[shape(2, CORE_ROWS, LANES)] * 2,
        in_specs=[anywhere] * 7,
        out_specs=[vmem] * 2,
        scratch_shapes=[
            pltpu.VMEM((ITEMS + 1, 4, ROWS + 2 * GUARD, LANES), F32),
            pltpu.VMEM((2, CORE_ROWS + TILE, LANES), F32),
            pltpu.VMEM((2, 2, stage_rows, LANES), F32),
        ]
        + scratch(ITEMS + 1, 3),
        compiler_params=SMALL,
    )(*inputs)
    received = across(send, 2)
    kept = pl.pallas_call(
        march_kept,
        out_shape=shape(2, CORE_ROWS, LANES),
        in_specs=[anywhere] * 7 + [vmem],
        out_specs=vmem,
        scratch_shapes=[
            pltpu.VMEM((2, 4, ROWS + 2 * GUARD, LANES), F32),
            pltpu.VMEM((2, stage_rows, LANES), F32),
        ]
        + scratch(2, 1),
        compiler_params=SMALL,
    )(*inputs, sums)
    return kept + received


def solution(mesh):
    return jax.shard_map(
        shards,
        mesh=mesh,
        in_specs=(
            P(None, "freq", None, "strip"),
            P(None, "freq", None, "strip"),
            P(None, "strip", None),
            P("freq"),
        ),
        out_specs=P(None, "freq", "strip"),
        check_vma=False,
    )
```

```python
import functools

import jax
import jax.numpy as jnp
from jax import lax
from jax.experimental import pallas as pl
from jax.experimental.pallas import tpu as pltpu
from jax.sharding import PartitionSpec as P

BLOCKS = 4
ITEMS = 4
LANES = 128
TILE = 8
WIN = 32
HALO = 4
CORE_ROWS = 128
ROWS = CORE_ROWS + 2 * TILE
GUARD = TILE
CHUNK = 72
SPAN = 9
GROUPS = 2

phase_depth = 2.0
fd_coef = 0.03

F32 = jnp.float32


def lanes_of(rows):
    return lax.broadcasted_iota(jnp.int32, (rows, LANES), 1)


def lane_roll(x, shift):
    return pltpu.roll(x, shift % LANES, 1)


def pack_speed(vel_ref, out_ref, held, packed, sems):
    core = lax.axis_index("freq") & 1
    strips = vel_ref.shape[2] // LANES
    group = strips // GROUPS
    width = group * LANES
    reads = []
    for step in range(GROUPS):
        columns = slice(step * width, (step + 1) * width)
        reads.append(
            pltpu.make_async_copy(
                vel_ref.at[core, :, columns], held.at[:, columns], sems.at[0, step]
            )
        )
        reads[step].start()
    dims = (group, TILE, LANES)
    lane = lax.broadcasted_iota(jnp.int32, dims, 2)
    sublane = lax.broadcasted_iota(jnp.int32, dims, 1)

    def strip_of(strip):
        strip = min(max(strip, 0), strips - 1)
        return held[:, strip * LANES : (strip + 1) * LANES]

    writes = []
    reads[0].wait()
    for step in range(GROUPS):
        if step + 1 < GROUPS:
            reads[step + 1].wait()
        span = [strip_of(step * group + i) for i in range(-1, group + 1)]
        left = pltpu.roll(jnp.stack(span[:group]), 2 * HALO, 2)
        beside = jnp.where(lane < HALO, jnp.stack(span[2:]), left)
        beside = jnp.where(lane < 2 * HALO, beside, 0.0)
        for shift in (16, 32, 64):
            beside = beside + pltpu.roll(beside, shift, 2)
        beside = jnp.where((lane >> 4) == 7 - sublane, beside, 0.0)
        beside = jnp.sum(beside, axis=1, keepdims=True)
        rows = slice(step * group * SPAN, (step + 1) * group * SPAN)
        out = packed.at[rows]
        for i in range(group):
            out[SPAN * i : SPAN * i + TILE, :] = span[i + 1]
            out[SPAN * i + TILE : SPAN * (i + 1), :] = beside[i]
        writes.append(
            pltpu.make_async_copy(packed.at[rows], out_ref.at[rows], sems.at[1, step])
        )
        writes[step].start()
    for write in writes:
        write.wait()


def first_row(block, rows):
    start = jnp.clip(block * CORE_ROWS - TILE, 0, rows - ROWS)
    return pl.multiple_of(start, TILE)


def cut_waves(src_any, rec_any, edges_ref, message_ref, src_ref, rec_ref, sems):
    copies, copy_in = copier(sems)
    copy_in(src_any, src_ref)
    copy_in(rec_any, rec_ref)
    other = 1 - (lax.axis_index("freq") & 1)
    for copy in copies:
        copy.wait()
    fields = (src_ref.at[0, 0], src_ref.at[1, 0], rec_ref.at[0, 0], rec_ref.at[1, 0])
    lane = lanes_of(CORE_ROWS)
    packed = jnp.zeros((CORE_ROWS, LANES), F32)
    for group in range(BLOCKS):
        for part, field in enumerate(fields):
            slot = 4 * group + part
            value = field[group * CORE_ROWS : (group + 1) * CORE_ROWS, :]
            packed = jnp.where((lane >> 3) == slot, lane_roll(value, 8 * slot + 4), packed)
    edges_ref[...] = jnp.where((lane & 7) < 4, lane_roll(packed, -4), lane_roll(packed, 4))
    for b in range(2):
        rows = pl.ds(first_row(2 * b + other, src_ref.shape[2]), ROWS)
        for part, field in enumerate(fields):
            message_ref[4 * b + part] = field[rows, :]


SIN_TERMS = (1.0, -0.166666641831398, 0.008333218283951283, -0.00019823516777250916, 2.643730113049969e-06)
COS_TERMS = (1.0, -0.5, 0.041666656732559204, -0.0013888673856854439, 2.4778757506283e-05, -2.6437069777784927e-07)


def horner(terms, x):
    value = terms[-1]
    for term in terms[-2::-1]:
        value = value * x + term
    return value


def sin_cos(x):
    t = 0.5 * x - 0.7853981633974483
    square = t * t
    sine = t * horner(SIN_TERMS, square)
    cosine = horner(COS_TERMS, square)
    twice = -2.0 * sine
    return 1.0 + twice * sine, twice * cosine


def stepper(waves, speed, coef, omega, first, second, images):
    chunks = ROWS // CHUNK
    guard = jnp.zeros((TILE, LANES), F32)
    for buffer in (first, second):
        for part in range(4):
            buffer[part, 0:GUARD, :] = guard
            buffer[part, GUARD + ROWS :, :] = guard
    images[...] = jnp.zeros_like(images)

    def turn(values, depth, kind, row, freq_row):
        theta = freq_row * speed[kind, depth, pl.ds(row, CHUNK), :]
        sine, cosine = sin_cos(theta)
        src_re, src_im, rec_re, rec_im = values
        return (
            src_re * cosine - src_im * sine,
            src_re * sine + src_im * cosine,
            rec_re * cosine + rec_im * sine,
            rec_im * cosine - rec_re * sine,
        )

    def substep(buffer, depth, kind, row, freq_inverse):
        step = coef[kind, depth, pl.ds(row, CHUNK), :] * freq_inverse
        centers = []
        laps = []
        for part in range(4):
            center = buffer[part, pl.ds(row + GUARD, CHUNK), :]
            up = buffer[part, pl.ds(row + GUARD - 1, CHUNK), :]
            down = buffer[part, pl.ds(row + GUARD + 1, CHUNK), :]
            across = lane_roll(center, 1) + lane_roll(center, LANES - 1)
            centers.append(center)
            laps.append((across + (up + down)) - 4.0 * center)
        src_re, src_im, rec_re, rec_im = centers
        return (
            src_re - step * laps[1],
            src_im + step * laps[0],
            rec_re + step * laps[3],
            rec_im - step * laps[2],
        )

    def store(buffer, row, values):
        for part in range(4):
            buffer[part, pl.ds(row + GUARD, CHUNK), :] = values[part]

    def product(values):
        return values[0] * values[2] + values[1] * values[3]

    def add_image(kind, depth, row, value):
        low, high = max(row, TILE), min(row + CHUNK, TILE + CORE_ROWS)
        if low < high:
            images[kind, depth, low - TILE : high - TILE, :] += value[low - row : high - row, :]

    def item(k, kind):
        freq_row = omega[pl.ds(pl.multiple_of(k * TILE, TILE), 1), :]
        freq_inverse = 1.0 / freq_row

        for j in range(chunks):
            row = j * CHUNK
            values = [waves[k, part, pl.ds(row + GUARD, CHUNK), :] for part in range(4)]
            store(first, row, turn(values, 0, kind, row, freq_row))
        for j in range(chunks):
            store(second, j * CHUNK, substep(first, 0, kind, j * CHUNK, freq_inverse))
        for j in range(chunks):
            row = j * CHUNK
            values = substep(second, 0, kind, row, freq_inverse)
            add_image(kind, 0, row, product(values))
            store(first, row, turn(values, 1, kind, row, freq_row))
        for j in range(chunks):
            store(second, j * CHUNK, substep(first, 1, kind, j * CHUNK, freq_inverse))
        for j in range(chunks):
            values = substep(second, 1, kind, j * CHUNK, freq_inverse)
            add_image(kind, 1, j * CHUNK, product(values))

    return item


def clear_above(waves, items):
    for m in items:
        for part in range(4):
            waves[m, part, GUARD : GUARD + TILE, :] = jnp.zeros((TILE, LANES), F32)


def clear_below(waves, items):
    for m in items:
        for part in range(4):
            rows = slice(GUARD + ROWS - TILE, GUARD + ROWS)
            waves[m, part, rows, :] = jnp.zeros((TILE, LANES), F32)


def copier(sems):
    copies = []

    def copy_in(source, target):
        copy = pltpu.make_async_copy(source, target, sems.at[len(copies)])
        copy.start()
        copies.append(copy)

    return copies, copy_in


def copy_speeds(copy_in, speed_refs, stage, block, core):
    block_rows = SPAN * (CORE_ROWS // TILE)
    mid = pl.multiple_of(block * block_rows, TILE)
    above = pl.multiple_of(jnp.maximum(mid - 16, 0), TILE)
    below = pl.multiple_of(jnp.minimum(mid + block_rows, speed_refs[0].shape[0] - 16), TILE)
    for which, speed_ref in enumerate(speed_refs):
        target = stage.at[core ^ which]
        copy_in(speed_ref.at[pl.ds(above, 16)], target.at[0:16])
        copy_in(speed_ref.at[pl.ds(mid, block_rows)], target.at[16 : 16 + block_rows])
        copy_in(speed_ref.at[pl.ds(below, 16)], target.at[16 + block_rows :])


def copy_waves(copy_in, src_ref, rec_ref, message_ref, waves, block, b, m):
    start = first_row(block, src_ref.shape[2])
    landing = pl.ds(pl.multiple_of(start - block * CORE_ROWS + GUARD + TILE, TILE), ROWS)
    rows = pl.ds(start, ROWS)
    copy_in(src_ref.at[:, 0, rows, :], waves.at[m, 0:2, landing, :])
    copy_in(rec_ref.at[:, 0, rows, :], waves.at[m, 2:4, landing, :])
    copy_in(message_ref.at[pl.ds(4 * b, 4)], waves.at[m + 1, :, landing, :])


def tile_speeds(stage, depth):
    tiles = ROWS // TILE
    return jnp.stack([stage[depth, 7 + SPAN * i : 15 + SPAN * i, :] for i in range(tiles)])


def patch(image, value, b):
    lane = lanes_of(CORE_ROWS)
    image = jnp.where(lane < HALO, pltpu.roll(value, (2 * LANES - 64 * b - 36) & 127, 1), image)
    return jnp.where(
        lane >= LANES - HALO, pltpu.roll(value, (LANES + 100 - 64 * b) & 127, 1), image
    )


def cut_windows(src_ref, rec_ref, message_ref, windows_ref, waves, sems):
    core = lax.axis_index("freq") & 1
    copies, copy_in = copier(sems)
    for b in range(2):
        copy_waves(copy_in, src_ref, rec_ref, message_ref, waves, 2 * b + core, b, 2 * b)
    for copy in copies:
        copy.wait()
    clear_ends(waves, core)
    lane = lanes_of(ROWS)
    place = lane & (WIN - 1)
    for part in range(4):
        own = waves[0, part, GUARD : GUARD + ROWS, :]
        for m in range(1, ITEMS):
            value = lane_roll(waves[m, part, GUARD : GUARD + ROWS, :], WIN * m)
            own = jnp.where((((lane + 16) >> 5) & 3) == m, value, own)
        windows_ref[part] = jnp.where(place < 16, lane_roll(own, 36), lane_roll(own, 28))


def clear_ends(waves, core):
    @pl.when(core == 0)
    def _():
        clear_above(waves, range(2))

    @pl.when(core == 1)
    def _():
        clear_below(waves, range(2, 4))


def march_sent(*refs):
    speed_refs, src_ref, rec_ref, message_ref, halo_refs = refs[:2], *refs[2:5], refs[5:7]
    windows_ref, send_ref, sums_ref = refs[7:10]
    waves, sides, stage, speed, coef, omega, first, second, images, sems = refs[10:]
    freq = lax.axis_index("freq")
    core = freq & 1
    strip = lax.axis_index("strip")
    strips = lax.axis_size("strip")
    copies, copy_in = copier(sems)
    for b in range(2):
        copy_speeds(copy_in, speed_refs, stage.at[b], 2 * b + core, core)
    speed_count = len(copies)
    for b in range(2):
        copy_waves(copy_in, src_ref, rec_ref, message_ref, waves, 2 * b + core, b, 2 * b)
    for k in range(2):
        copy_in(halo_refs[k], sides.at[k])
    copy_in(windows_ref, waves.at[ITEMS, :, GUARD : GUARD + ROWS, :])

    item = stepper(waves, speed, coef, omega, first, second, images)
    for copy in copies[:speed_count]:
        copy.wait()
    tiles = ROWS // TILE
    dims = (tiles, TILE, LANES)
    lane = lax.broadcasted_iota(jnp.int32, dims, 2)
    place = lane & (WIN - 1)
    tile = lax.broadcasted_iota(jnp.int32, dims, 0)
    on_grid = jnp.logical_not(
        ((place < 4) & (strip == 0)) | ((place >= 28) & (strip == strips - 1))
    )
    for depth in range(2):
        window = jnp.zeros(dims, F32)
        window_live = place < 0
        for b in range(2):
            block = 2 * b + core
            live = jnp.logical_not(
                ((tile == 0) & (block == 0)) | ((tile == tiles - 1) & (block == BLOCKS - 1))
            )
            here = tile_speeds(stage.at[b], depth)
            beside = jnp.stack(
                [
                    jnp.broadcast_to(
                        stage[b, depth, 15 + SPAN * i : 16 + SPAN * i, :], (TILE, LANES)
                    )
                    for i in range(tiles)
                ]
            )
            beside = pltpu.roll(beside, 0, 2, stride=16, stride_axis=1)
            base = 64 * b

            def lanes_in(low, high):
                return (lane >= base + low) & (lane < base + high)

            window = jnp.where(
                lanes_in(16, 28), pltpu.roll(here, (base + 28) % LANES, 2), window
            )
            window = jnp.where(
                lanes_in(28, 36), pltpu.roll(beside, (base + 44) % LANES, 2), window
            )
            window = jnp.where(
                lanes_in(36, 48), pltpu.roll(here, (base + 36) % LANES, 2), window
            )
            window_live = window_live | (live & ((((lane + 112) >> 6) & 1) == b))
            speed[b, depth] = (phase_depth / here).reshape(ROWS, LANES)
            coef[b, depth] = jnp.where(live, fd_coef * here, 0.0).reshape(ROWS, LANES)
        window = window + pltpu.roll(window, WIN, 2)
        speed[2, depth] = (phase_depth / window).reshape(ROWS, LANES)
        coef[2, depth] = jnp.where(
            on_grid & window_live, fd_coef * window, 0.0
        ).reshape(ROWS, LANES)

    for copy in copies[speed_count:]:
        copy.wait()

    clear_ends(waves, core)

    def turned(k, low, high, shift):
        return pltpu.roll(sides[k, low:high, :], (WIN * (shift - core)) & (LANES - 1), 1)

    def pick(low, high, shift):
        odd = ((lanes_of(high - low) >> 5) & 1) == 1
        return jnp.where(odd, turned(1, low, high, shift + 1), turned(0, low, high, shift))

    tile_lane = lanes_of(TILE)
    above = pick(CORE_ROWS - TILE, CORE_ROWS, 1)
    above = jnp.where((tile_lane < 2 * WIN) & (core == 0), 0.0, above)
    below = pick(0, TILE, LANES // WIN - 1)
    below = jnp.where((tile_lane >= 2 * WIN) & (core == 1), 0.0, below)
    beside = jnp.concatenate([above, pick(0, CORE_ROWS, 0), below])
    place = lanes_of(ROWS) & (WIN - 1)
    halo = (place < 4) | (place >= 28)
    for part in range(4):
        window = waves[ITEMS, part, GUARD : GUARD + ROWS, :]
        waves[ITEMS, part, GUARD : GUARD + ROWS, :] = jnp.where(
            halo, lane_roll(beside, 28 - 8 * part), window
        )
    rows = [sides[k, CORE_ROWS : CORE_ROWS + TILE, :] for k in range(2)]
    odd = (((tile_lane + 112) >> 5) & 1) == 1
    for m in range(ITEMS):
        omega[m * TILE : (m + 1) * TILE, :] = rows[m & 1]
    omega[ITEMS * TILE :, :] = jnp.where(odd, rows[1], rows[0])

    sent = 1 - (freq >> 1)

    def step(j, carry):
        k = jnp.where(j == 2, ITEMS, 2 * sent + j)
        item(k, k >> 1)
        return carry

    lax.fori_loop(0, 3, step, 0)
    for depth in range(2):
        value = images[2, depth]
        value = value + lane_roll(value, -WIN)
        sums_ref[depth] = value
        send_ref[depth] = patch(images[sent, depth], value, sent)


def march_kept(*refs):
    speed_refs, src_ref, rec_ref, message_ref, halo_refs = refs[:2], *refs[2:5], refs[5:7]
    sums_ref, image_ref = refs[7:9]
    waves, stage, speed, coef, omega, first, second, images, sems = refs[9:]
    freq = lax.axis_index("freq")
    core = freq & 1
    b = freq >> 1
    copies, copy_in = copier(sems)
    copy_speeds(copy_in, speed_refs, stage, freq, core)
    copy_waves(copy_in, src_ref, rec_ref, message_ref, waves, freq, b, 0)
    for k in range(2):
        copy_in(
            halo_refs[k].at[CORE_ROWS : CORE_ROWS + TILE], omega.at[k * TILE : (k + 1) * TILE]
        )
    item = stepper(waves, speed, coef, omega, first, second, images)
    for copy in copies:
        copy.wait()
    tiles = ROWS // TILE
    tile = lax.broadcasted_iota(jnp.int32, (tiles, TILE, LANES), 0)
    live = jnp.logical_not(
        ((tile == 0) & (freq == 0)) | ((tile == tiles - 1) & (freq == BLOCKS - 1))
    )
    for depth in range(2):
        here = tile_speeds(stage, depth)
        speed[0, depth] = (phase_depth / here).reshape(ROWS, LANES)
        coef[0, depth] = jnp.where(live, fd_coef * here, 0.0).reshape(ROWS, LANES)

    @pl.when(freq == 0)
    def _():
        clear_above(waves, range(2))

    @pl.when(freq == BLOCKS - 1)
    def _():
        clear_below(waves, range(2))

    def step(k, carry):
        item(k, 0)
        return carry

    lax.fori_loop(0, 2, step, 0)
    for depth in range(2):
        image_ref[depth] = patch(images[0, depth], sums_ref[depth], b)


SMALL = pltpu.CompilerParams(vmem_limit_bytes=16 * 1024 * 1024)


def shape(*dims):
    return jax.ShapeDtypeStruct(dims, F32)


def shards(source, receiver, velocity, omega):
    strips = lax.axis_size("strip")
    freqs = lax.axis_size("freq")
    vmem = pl.BlockSpec(memory_space=pltpu.VMEM)
    anywhere = pl.BlockSpec(memory_space=pl.ANY)

    def across(x, k):
        return lax.ppermute(x, "freq", [(i, i ^ k) for i in range(freqs)])

    packed = pl.pallas_call(
        pack_speed,
        out_shape=shape(SPAN * strips, LANES),
        in_specs=[anywhere],
        out_specs=anywhere,
        scratch_shapes=[
            pltpu.VMEM((TILE, strips * LANES), F32),
            pltpu.VMEM((SPAN * strips, LANES), F32),
            pltpu.SemaphoreType.DMA((2, GROUPS)),
        ],
    )(velocity)
    speeds = lax.all_to_all(
        packed.reshape(strips, 1, SPAN * LANES), "strip", split_axis=0, concat_axis=0, tiled=True
    ).reshape(SPAN * strips, LANES)
    other_speeds = across(speeds, 1)

    edges, message = pl.pallas_call(
        cut_waves,
        out_shape=[shape(CORE_ROWS, LANES), shape(8, ROWS, LANES)],
        in_specs=[anywhere, anywhere],
        out_specs=[vmem, vmem],
        scratch_shapes=[pltpu.VMEM(source.shape, F32)] * 2 + [pltpu.SemaphoreType.DMA((2,))],
        compiler_params=SMALL,
    )(source, receiver)
    def swap(x, pairs):
        return lax.ppermute(x, "strip", [p for i, j in pairs for p in ((i, j), (j, i))])

    with_far = swap(edges, [(i, i + 1) for i in range(1, strips - 1, 2)])
    with_near = swap(edges, [(i, i + 1) for i in range(0, strips, 2)])
    message = across(message, 1)
    parity = lax.axis_index("strip") & 1
    from_near = (((lanes_of(CORE_ROWS) >> 2) ^ parity) & 1) == 0
    halos = jnp.concatenate(
        [
            jnp.where(from_near, with_near, with_far),
            jnp.broadcast_to(omega[:, None], (TILE, LANES)),
        ]
    )

    windows = pl.pallas_call(
        cut_windows,
        out_shape=shape(4, ROWS, LANES),
        in_specs=[anywhere] * 3,
        out_specs=vmem,
        scratch_shapes=[
            pltpu.VMEM((ITEMS, 4, ROWS + 2 * GUARD, LANES), F32),
            pltpu.SemaphoreType.DMA((6,)),
        ],
        compiler_params=SMALL,
    )(source, receiver, message)
    inputs = (speeds, other_speeds, source, receiver, message, halos, across(halos, 1))

    def scratch(items, kinds):
        return [
            pltpu.VMEM((kinds, 2, ROWS, LANES), F32),
            pltpu.VMEM((kinds, 2, ROWS, LANES), F32),
            pltpu.VMEM((items * TILE, LANES), F32),
            pltpu.VMEM((4, ROWS + 2 * GUARD, LANES), F32),
            pltpu.VMEM((4, ROWS + 2 * GUARD, LANES), F32),
            pltpu.VMEM((kinds, 2, CORE_ROWS, LANES), F32),
            pltpu.SemaphoreType.DMA((21,)),
        ]

    stage_rows = 32 + SPAN * CORE_ROWS // TILE
    send, sums = pl.pallas_call(
        march_sent,
        out_shape=[shape(2, CORE_ROWS, LANES)] * 2,
        in_specs=[anywhere] * 8,
        out_specs=[vmem] * 2,
        scratch_shapes=[
            pltpu.VMEM((ITEMS + 1, 4, ROWS + 2 * GUARD, LANES), F32),
            pltpu.VMEM((2, CORE_ROWS + TILE, LANES), F32),
            pltpu.VMEM((2, 2, stage_rows, LANES), F32),
        ]
        + scratch(ITEMS + 1, 3),
        compiler_params=SMALL,
    )(*inputs, windows)
    received = across(send, 2)
    kept = pl.pallas_call(
        march_kept,
        out_shape=shape(2, CORE_ROWS, LANES),
        in_specs=[anywhere] * 7 + [vmem],
        out_specs=vmem,
        scratch_shapes=[
            pltpu.VMEM((2, 4, ROWS + 2 * GUARD, LANES), F32),
            pltpu.VMEM((2, stage_rows, LANES), F32),
        ]
        + scratch(2, 1),
        compiler_params=SMALL,
    )(*inputs, sums)
    return kept + received


def solution(mesh):
    return jax.shard_map(
        shards,
        mesh=mesh,
        in_specs=(
            P(None, "freq", None, "strip"),
            P(None, "freq", None, "strip"),
            P(None, "strip", None),
            P("freq"),
        ),
        out_specs=P(None, "freq", "strip"),
        check_vma=False,
    )
```

```python
import functools

import jax
import jax.numpy as jnp
from jax import lax
from jax.experimental import pallas as pl
from jax.experimental.pallas import tpu as pltpu
from jax.sharding import PartitionSpec as P

BLOCKS = 4
ITEMS = 4
LANES = 128
TILE = 8
WIN = 32
HALO = 4
CORE_ROWS = 128
ROWS = CORE_ROWS + 2 * TILE
GUARD = TILE
CHUNK = 72
SPAN = 9
GROUPS = 2

phase_depth = 2.0
fd_coef = 0.03

F32 = jnp.float32


def lanes_of(rows):
    return lax.broadcasted_iota(jnp.int32, (rows, LANES), 1)


def lane_roll(x, shift):
    return pltpu.roll(x, shift % LANES, 1)


def pack_speed(vel_ref, out_ref, held, packed, sems):
    core = lax.axis_index("freq") & 1
    strips = vel_ref.shape[2] // LANES
    group = strips // GROUPS
    width = group * LANES
    reads = []
    for step in range(GROUPS):
        columns = slice(step * width, (step + 1) * width)
        reads.append(
            pltpu.make_async_copy(
                vel_ref.at[core, :, columns], held.at[:, columns], sems.at[0, step]
            )
        )
        reads[step].start()
    dims = (group, TILE, LANES)
    lane = lax.broadcasted_iota(jnp.int32, dims, 2)
    sublane = lax.broadcasted_iota(jnp.int32, dims, 1)

    def strip_of(strip):
        strip = min(max(strip, 0), strips - 1)
        return held[:, strip * LANES : (strip + 1) * LANES]

    writes = []
    reads[0].wait()
    for step in range(GROUPS):
        if step + 1 < GROUPS:
            reads[step + 1].wait()
        span = [strip_of(step * group + i) for i in range(-1, group + 1)]
        left = pltpu.roll(jnp.stack(span[:group]), 2 * HALO, 2)
        beside = jnp.where(lane < HALO, jnp.stack(span[2:]), left)
        beside = jnp.where(lane < 2 * HALO, beside, 0.0)
        for shift in (16, 32, 64):
            beside = beside + pltpu.roll(beside, shift, 2)
        beside = jnp.where((lane >> 4) == 7 - sublane, beside, 0.0)
        beside = jnp.sum(beside, axis=1, keepdims=True)
        rows = slice(step * group * SPAN, (step + 1) * group * SPAN)
        out = packed.at[rows]
        for i in range(group):
            out[SPAN * i : SPAN * i + TILE, :] = span[i + 1]
            out[SPAN * i + TILE : SPAN * (i + 1), :] = beside[i]
        writes.append(
            pltpu.make_async_copy(packed.at[rows], out_ref.at[rows], sems.at[1, step])
        )
        writes[step].start()
    for write in writes:
        write.wait()


def first_row(block, rows):
    start = jnp.clip(block * CORE_ROWS - TILE, 0, rows - ROWS)
    return pl.multiple_of(start, TILE)


def cut_waves(src_any, rec_any, edges_ref, message_ref, src_ref, rec_ref, sems):
    copies, copy_in = copier(sems)
    copy_in(src_any, src_ref)
    copy_in(rec_any, rec_ref)
    other = 1 - (lax.axis_index("freq") & 1)
    for copy in copies:
        copy.wait()
    fields = (src_ref.at[0, 0], src_ref.at[1, 0], rec_ref.at[0, 0], rec_ref.at[1, 0])
    lane = lanes_of(CORE_ROWS)
    packed = jnp.zeros((CORE_ROWS, LANES), F32)
    for group in range(BLOCKS):
        for part, field in enumerate(fields):
            slot = 4 * group + part
            value = field[group * CORE_ROWS : (group + 1) * CORE_ROWS, :]
            packed = jnp.where((lane >> 3) == slot, lane_roll(value, 8 * slot + 4), packed)
    edges_ref[...] = jnp.where((lane & 7) < 4, lane_roll(packed, -4), lane_roll(packed, 4))
    for b in range(2):
        rows = pl.ds(first_row(2 * b + other, src_ref.shape[2]), ROWS)
        for part, field in enumerate(fields):
            message_ref[4 * b + part] = field[rows, :]


SIN_TERMS = (1.0, -0.166666641831398, 0.008333218283951283, -0.00019823516777250916, 2.643730113049969e-06)
COS_TERMS = (1.0, -0.5, 0.041666656732559204, -0.0013888673856854439, 2.4778757506283e-05, -2.6437069777784927e-07)


def horner(terms, x):
    value = terms[-1]
    for term in terms[-2::-1]:
        value = value * x + term
    return value


def sin_cos(x):
    t = 0.5 * x - 0.7853981633974483
    square = t * t
    sine = t * horner(SIN_TERMS, square)
    cosine = horner(COS_TERMS, square)
    twice = -2.0 * sine
    return 1.0 + twice * sine, twice * cosine


def stepper(waves, speed, coef, omega, first, second, images):
    chunks = ROWS // CHUNK
    guard = jnp.zeros((TILE, LANES), F32)
    for buffer in (first, second):
        for part in range(4):
            buffer[part, 0:GUARD, :] = guard
            buffer[part, GUARD + ROWS :, :] = guard
    images[...] = jnp.zeros_like(images)

    def turn(values, depth, kind, row, freq_row):
        theta = freq_row * speed[kind, depth, pl.ds(row, CHUNK), :]
        sine, cosine = sin_cos(theta)
        src_re, src_im, rec_re, rec_im = values
        return (
            src_re * cosine - src_im * sine,
            src_re * sine + src_im * cosine,
            rec_re * cosine + rec_im * sine,
            rec_im * cosine - rec_re * sine,
        )

    def substep(buffer, depth, kind, row, freq_inverse):
        step = coef[kind, depth, pl.ds(row, CHUNK), :] * freq_inverse
        centers = []
        laps = []
        for part in range(4):
            center = buffer[part, pl.ds(row + GUARD, CHUNK), :]
            up = buffer[part, pl.ds(row + GUARD - 1, CHUNK), :]
            down = buffer[part, pl.ds(row + GUARD + 1, CHUNK), :]
            across = lane_roll(center, 1) + lane_roll(center, LANES - 1)
            centers.append(center)
            laps.append((across + (up + down)) - 4.0 * center)
        src_re, src_im, rec_re, rec_im = centers
        return (
            src_re - step * laps[1],
            src_im + step * laps[0],
            rec_re + step * laps[3],
            rec_im - step * laps[2],
        )

    def store(buffer, row, values):
        for part in range(4):
            buffer[part, pl.ds(row + GUARD, CHUNK), :] = values[part]

    def product(values):
        return values[0] * values[2] + values[1] * values[3]

    def add_image(kind, depth, row, value):
        low, high = max(row, TILE), min(row + CHUNK, TILE + CORE_ROWS)
        if low < high:
            images[kind, depth, low - TILE : high - TILE, :] += value[low - row : high - row, :]

    def item(k, kind):
        freq_row = omega[pl.ds(pl.multiple_of(k * TILE, TILE), 1), :]
        freq_inverse = 1.0 / freq_row

        for j in range(chunks):
            row = j * CHUNK
            values = [waves[k, part, pl.ds(row + GUARD, CHUNK), :] for part in range(4)]
            store(first, row, turn(values, 0, kind, row, freq_row))
        for j in range(chunks):
            store(second, j * CHUNK, substep(first, 0, kind, j * CHUNK, freq_inverse))
        for j in range(chunks):
            row = j * CHUNK
            values = substep(second, 0, kind, row, freq_inverse)
            add_image(kind, 0, row, product(values))
            store(first, row, turn(values, 1, kind, row, freq_row))
        for j in range(chunks):
            store(second, j * CHUNK, substep(first, 1, kind, j * CHUNK, freq_inverse))
        for j in range(chunks):
            values = substep(second, 1, kind, j * CHUNK, freq_inverse)
            add_image(kind, 1, j * CHUNK, product(values))

    return item


def clear_above(waves, items):
    for m in items:
        for part in range(4):
            waves[m, part, GUARD : GUARD + TILE, :] = jnp.zeros((TILE, LANES), F32)


def clear_below(waves, items):
    for m in items:
        for part in range(4):
            rows = slice(GUARD + ROWS - TILE, GUARD + ROWS)
            waves[m, part, rows, :] = jnp.zeros((TILE, LANES), F32)


def copier(sems):
    copies = []

    def copy_in(source, target):
        copy = pltpu.make_async_copy(source, target, sems.at[len(copies)])
        copy.start()
        copies.append(copy)

    return copies, copy_in


def copy_speeds(copy_in, speed_refs, stage, block, core):
    block_rows = SPAN * (CORE_ROWS // TILE)
    mid = pl.multiple_of(block * block_rows, TILE)
    above = pl.multiple_of(jnp.maximum(mid - 16, 0), TILE)
    below = pl.multiple_of(jnp.minimum(mid + block_rows, speed_refs[0].shape[0] - 16), TILE)
    for which, speed_ref in enumerate(speed_refs):
        target = stage.at[core ^ which]
        copy_in(speed_ref.at[pl.ds(above, 16)], target.at[0:16])
        copy_in(speed_ref.at[pl.ds(mid, block_rows)], target.at[16 : 16 + block_rows])
        copy_in(speed_ref.at[pl.ds(below, 16)], target.at[16 + block_rows :])


def copy_waves(copy_in, src_ref, rec_ref, message_ref, waves, block, b, m):
    start = first_row(block, src_ref.shape[2])
    landing = pl.ds(pl.multiple_of(start - block * CORE_ROWS + GUARD + TILE, TILE), ROWS)
    rows = pl.ds(start, ROWS)
    copy_in(src_ref.at[:, 0, rows, :], waves.at[m, 0:2, landing, :])
    copy_in(rec_ref.at[:, 0, rows, :], waves.at[m, 2:4, landing, :])
    copy_in(message_ref.at[pl.ds(4 * b, 4)], waves.at[m + 1, :, landing, :])


def tile_speeds(stage, depth):
    tiles = ROWS // TILE
    return jnp.stack([stage[depth, 7 + SPAN * i : 15 + SPAN * i, :] for i in range(tiles)])


def patch(image, value, b):
    lane = lanes_of(CORE_ROWS)
    image = jnp.where(lane < HALO, pltpu.roll(value, (2 * LANES - 64 * b - 36) & 127, 1), image)
    return jnp.where(
        lane >= LANES - HALO, pltpu.roll(value, (LANES + 100 - 64 * b) & 127, 1), image
    )


def cut_windows(src_ref, rec_ref, message_ref, windows_ref, waves, sems):
    core = lax.axis_index("freq") & 1
    copies, copy_in = copier(sems)
    for b in range(2):
        copy_waves(copy_in, src_ref, rec_ref, message_ref, waves, 2 * b + core, b, 2 * b)
    for copy in copies:
        copy.wait()
    clear_ends(waves, core)
    lane = lanes_of(ROWS)
    place = lane & (WIN - 1)
    for part in range(4):
        own = waves[0, part, GUARD : GUARD + ROWS, :]
        for m in range(1, ITEMS):
            value = lane_roll(waves[m, part, GUARD : GUARD + ROWS, :], WIN * m)
            own = jnp.where((((lane + 16) >> 5) & 3) == m, value, own)
        windows_ref[part] = jnp.where(place < 16, lane_roll(own, 36), lane_roll(own, 28))


def clear_ends(waves, core):
    @pl.when(core == 0)
    def _():
        clear_above(waves, range(2))

    @pl.when(core == 1)
    def _():
        clear_below(waves, range(2, 4))


def march_sent(*refs):
    speed_refs, src_ref, rec_ref, message_ref, halo_refs = refs[:2], *refs[2:5], refs[5:7]
    windows_ref, send_ref, sums_ref = refs[7:10]
    waves, sides, stage, speed, coef, omega, first, second, images, sems = refs[10:]
    freq = lax.axis_index("freq")
    core = freq & 1
    strip = lax.axis_index("strip")
    strips = lax.axis_size("strip")
    copies, copy_in = copier(sems)
    for b in range(2):
        copy_speeds(copy_in, speed_refs, stage.at[b], 2 * b + core, core)
    speed_count = len(copies)
    sent = 1 - (freq >> 1)
    sent_block = 2 * sent + core
    copy_waves(copy_in, src_ref, rec_ref, message_ref, waves, sent_block, sent, 0)
    for k in range(2):
        copy_in(halo_refs[k], sides.at[k])
    copy_in(windows_ref, waves.at[2, :, GUARD : GUARD + ROWS, :])

    item = stepper(waves, speed, coef, omega, first, second, images)
    for copy in copies[:speed_count]:
        copy.wait()
    tiles = ROWS // TILE
    dims = (tiles, TILE, LANES)
    lane = lax.broadcasted_iota(jnp.int32, dims, 2)
    place = lane & (WIN - 1)
    tile = lax.broadcasted_iota(jnp.int32, dims, 0)
    on_grid = jnp.logical_not(
        ((place < 4) & (strip == 0)) | ((place >= 28) & (strip == strips - 1))
    )
    sent_live = jnp.logical_not(
        ((tile == 0) & (sent_block == 0)) | ((tile == tiles - 1) & (sent_block == BLOCKS - 1))
    )
    for depth in range(2):
        window = jnp.zeros(dims, F32)
        window_live = place < 0
        for b in range(2):
            block = 2 * b + core
            live = jnp.logical_not(
                ((tile == 0) & (block == 0)) | ((tile == tiles - 1) & (block == BLOCKS - 1))
            )
            here = tile_speeds(stage.at[b], depth)
            beside = jnp.stack(
                [
                    jnp.broadcast_to(
                        stage[b, depth, 15 + SPAN * i : 16 + SPAN * i, :], (TILE, LANES)
                    )
                    for i in range(tiles)
                ]
            )
            beside = pltpu.roll(beside, 0, 2, stride=16, stride_axis=1)
            base = 64 * b

            def lanes_in(low, high):
                return (lane >= base + low) & (lane < base + high)

            window = jnp.where(
                lanes_in(16, 28), pltpu.roll(here, (base + 28) % LANES, 2), window
            )
            window = jnp.where(
                lanes_in(28, 36), pltpu.roll(beside, (base + 44) % LANES, 2), window
            )
            window = jnp.where(
                lanes_in(36, 48), pltpu.roll(here, (base + 36) % LANES, 2), window
            )
            window_live = window_live | (live & ((((lane + 112) >> 6) & 1) == b))
        window = window + pltpu.roll(window, WIN, 2)
        here = tile_speeds(stage.at[sent], depth)
        speed[0, depth] = (phase_depth / here).reshape(ROWS, LANES)
        coef[0, depth] = jnp.where(sent_live, fd_coef * here, 0.0).reshape(ROWS, LANES)
        speed[1, depth] = (phase_depth / window).reshape(ROWS, LANES)
        coef[1, depth] = jnp.where(
            on_grid & window_live, fd_coef * window, 0.0
        ).reshape(ROWS, LANES)

    for copy in copies[speed_count:]:
        copy.wait()

    @pl.when(sent_block == 0)
    def _():
        clear_above(waves, range(2))

    @pl.when(sent_block == BLOCKS - 1)
    def _():
        clear_below(waves, range(2))

    def turned(k, low, high, shift):
        return pltpu.roll(sides[k, low:high, :], (WIN * (shift - core)) & (LANES - 1), 1)

    def pick(low, high, shift):
        odd = ((lanes_of(high - low) >> 5) & 1) == 1
        return jnp.where(odd, turned(1, low, high, shift + 1), turned(0, low, high, shift))

    tile_lane = lanes_of(TILE)
    above = pick(CORE_ROWS - TILE, CORE_ROWS, 1)
    above = jnp.where((tile_lane < 2 * WIN) & (core == 0), 0.0, above)
    below = pick(0, TILE, LANES // WIN - 1)
    below = jnp.where((tile_lane >= 2 * WIN) & (core == 1), 0.0, below)
    beside = jnp.concatenate([above, pick(0, CORE_ROWS, 0), below])
    place = lanes_of(ROWS) & (WIN - 1)
    halo = (place < 4) | (place >= 28)
    for part in range(4):
        window = waves[2, part, GUARD : GUARD + ROWS, :]
        waves[2, part, GUARD : GUARD + ROWS, :] = jnp.where(
            halo, lane_roll(beside, 28 - 8 * part), window
        )
    rows = [sides[k, CORE_ROWS : CORE_ROWS + TILE, :] for k in range(2)]
    odd = (((tile_lane + 112) >> 5) & 1) == 1
    for k in range(2):
        omega[k * TILE : (k + 1) * TILE, :] = rows[k]
    omega[2 * TILE :, :] = jnp.where(odd, rows[1], rows[0])

    def step(k, carry):
        item(k, k >> 1)
        return carry

    lax.fori_loop(0, 3, step, 0)
    for depth in range(2):
        value = images[1, depth]
        value = value + lane_roll(value, -WIN)
        sums_ref[depth] = value
        send_ref[depth] = patch(images[0, depth], value, sent)


def march_kept(*refs):
    speed_refs, src_ref, rec_ref, message_ref, halo_refs = refs[:2], *refs[2:5], refs[5:7]
    sums_ref, image_ref = refs[7:9]
    waves, stage, speed, coef, omega, first, second, images, sems = refs[9:]
    freq = lax.axis_index("freq")
    core = freq & 1
    b = freq >> 1
    copies, copy_in = copier(sems)
    copy_speeds(copy_in, speed_refs, stage, freq, core)
    copy_waves(copy_in, src_ref, rec_ref, message_ref, waves, freq, b, 0)
    for k in range(2):
        copy_in(
            halo_refs[k].at[CORE_ROWS : CORE_ROWS + TILE], omega.at[k * TILE : (k + 1) * TILE]
        )
    item = stepper(waves, speed, coef, omega, first, second, images)
    for copy in copies:
        copy.wait()
    tiles = ROWS // TILE
    tile = lax.broadcasted_iota(jnp.int32, (tiles, TILE, LANES), 0)
    live = jnp.logical_not(
        ((tile == 0) & (freq == 0)) | ((tile == tiles - 1) & (freq == BLOCKS - 1))
    )
    for depth in range(2):
        here = tile_speeds(stage, depth)
        speed[0, depth] = (phase_depth / here).reshape(ROWS, LANES)
        coef[0, depth] = jnp.where(live, fd_coef * here, 0.0).reshape(ROWS, LANES)

    @pl.when(freq == 0)
    def _():
        clear_above(waves, range(2))

    @pl.when(freq == BLOCKS - 1)
    def _():
        clear_below(waves, range(2))

    def step(k, carry):
        item(k, 0)
        return carry

    lax.fori_loop(0, 2, step, 0)
    for depth in range(2):
        image_ref[depth] = patch(images[0, depth], sums_ref[depth], b)


SMALL = pltpu.CompilerParams(vmem_limit_bytes=16 * 1024 * 1024)


def shape(*dims):
    return jax.ShapeDtypeStruct(dims, F32)


def shards(source, receiver, velocity, omega):
    strips = lax.axis_size("strip")
    freqs = lax.axis_size("freq")
    vmem = pl.BlockSpec(memory_space=pltpu.VMEM)
    anywhere = pl.BlockSpec(memory_space=pl.ANY)

    def across(x, k):
        return lax.ppermute(x, "freq", [(i, i ^ k) for i in range(freqs)])

    packed = pl.pallas_call(
        pack_speed,
        out_shape=shape(SPAN * strips, LANES),
        in_specs=[anywhere],
        out_specs=anywhere,
        scratch_shapes=[
            pltpu.VMEM((TILE, strips * LANES), F32),
            pltpu.VMEM((SPAN * strips, LANES), F32),
            pltpu.SemaphoreType.DMA((2, GROUPS)),
        ],
    )(velocity)
    speeds = lax.all_to_all(
        packed.reshape(strips, 1, SPAN * LANES), "strip", split_axis=0, concat_axis=0, tiled=True
    ).reshape(SPAN * strips, LANES)
    other_speeds = across(speeds, 1)

    edges, message = pl.pallas_call(
        cut_waves,
        out_shape=[shape(CORE_ROWS, LANES), shape(8, ROWS, LANES)],
        in_specs=[anywhere, anywhere],
        out_specs=[vmem, vmem],
        scratch_shapes=[pltpu.VMEM(source.shape, F32)] * 2 + [pltpu.SemaphoreType.DMA((2,))],
        compiler_params=SMALL,
    )(source, receiver)
    def swap(x, pairs):
        return lax.ppermute(x, "strip", [p for i, j in pairs for p in ((i, j), (j, i))])

    with_far = swap(edges, [(i, i + 1) for i in range(1, strips - 1, 2)])
    with_near = swap(edges, [(i, i + 1) for i in range(0, strips, 2)])
    message = across(message, 1)
    parity = lax.axis_index("strip") & 1
    from_near = (((lanes_of(CORE_ROWS) >> 2) ^ parity) & 1) == 0
    halos = jnp.concatenate(
        [
            jnp.where(from_near, with_near, with_far),
            jnp.broadcast_to(omega[:, None], (TILE, LANES)),
        ]
    )

    windows = pl.pallas_call(
        cut_windows,
        out_shape=shape(4, ROWS, LANES),
        in_specs=[anywhere] * 3,
        out_specs=vmem,
        scratch_shapes=[
            pltpu.VMEM((ITEMS, 4, ROWS + 2 * GUARD, LANES), F32),
            pltpu.SemaphoreType.DMA((6,)),
        ],
        compiler_params=SMALL,
    )(source, receiver, message)
    inputs = (speeds, other_speeds, source, receiver, message, halos, across(halos, 1))

    def scratch(items, kinds):
        return [
            pltpu.VMEM((kinds, 2, ROWS, LANES), F32),
            pltpu.VMEM((kinds, 2, ROWS, LANES), F32),
            pltpu.VMEM((items * TILE, LANES), F32),
            pltpu.VMEM((4, ROWS + 2 * GUARD, LANES), F32),
            pltpu.VMEM((4, ROWS + 2 * GUARD, LANES), F32),
            pltpu.VMEM((kinds, 2, CORE_ROWS, LANES), F32),
            pltpu.SemaphoreType.DMA((21,)),
        ]

    stage_rows = 32 + SPAN * CORE_ROWS // TILE
    send, sums = pl.pallas_call(
        march_sent,
        out_shape=[shape(2, CORE_ROWS, LANES)] * 2,
        in_specs=[anywhere] * 8,
        out_specs=[vmem] * 2,
        scratch_shapes=[
            pltpu.VMEM((3, 4, ROWS + 2 * GUARD, LANES), F32),
            pltpu.VMEM((2, CORE_ROWS + TILE, LANES), F32),
            pltpu.VMEM((2, 2, stage_rows, LANES), F32),
        ]
        + scratch(3, 2),
        compiler_params=SMALL,
    )(*inputs, windows)
    received = across(send, 2)
    kept = pl.pallas_call(
        march_kept,
        out_shape=shape(2, CORE_ROWS, LANES),
        in_specs=[anywhere] * 7 + [vmem],
        out_specs=vmem,
        scratch_shapes=[
            pltpu.VMEM((2, 4, ROWS + 2 * GUARD, LANES), F32),
            pltpu.VMEM((2, stage_rows, LANES), F32),
        ]
        + scratch(2, 1),
        compiler_params=SMALL,
    )(*inputs, sums)
    return kept + received


def solution(mesh):
    return jax.shard_map(
        shards,
        mesh=mesh,
        in_specs=(
            P(None, "freq", None, "strip"),
            P(None, "freq", None, "strip"),
            P(None, "strip", None),
            P("freq"),
        ),
        out_specs=P(None, "freq", "strip"),
        check_vma=False,
    )
```

```python
import functools

import jax
import jax.numpy as jnp
from jax import lax
from jax.experimental import pallas as pl
from jax.experimental.pallas import tpu as pltpu
from jax.sharding import PartitionSpec as P

BLOCKS = 4
ITEMS = 4
LANES = 128
TILE = 8
WIN = 32
HALO = 4
CORE_ROWS = 128
ROWS = CORE_ROWS + 2 * TILE
GUARD = TILE
CHUNK = 48
SPAN = 9
GROUPS = 2

half_depth = 1.0
fd_coef = 0.03

F32 = jnp.float32


def lanes_of(rows):
    return lax.broadcasted_iota(jnp.int32, (rows, LANES), 1)


def lane_roll(x, shift):
    return pltpu.roll(x, shift % LANES, 1)


def pack_speed(vel_ref, out_ref, held, packed, sems):
    core = lax.axis_index("freq") & 1
    strips = vel_ref.shape[2] // LANES
    group = strips // GROUPS
    width = group * LANES
    reads = []
    for step in range(GROUPS):
        columns = slice(step * width, (step + 1) * width)
        reads.append(
            pltpu.make_async_copy(
                vel_ref.at[core, :, columns], held.at[:, columns], sems.at[0, step]
            )
        )
        reads[step].start()
    dims = (group, TILE, LANES)
    lane = lax.broadcasted_iota(jnp.int32, dims, 2)
    sublane = lax.broadcasted_iota(jnp.int32, dims, 1)

    def strip_of(strip):
        strip = min(max(strip, 0), strips - 1)
        return held[:, strip * LANES : (strip + 1) * LANES]

    writes = []
    reads[0].wait()
    for step in range(GROUPS):
        if step + 1 < GROUPS:
            reads[step + 1].wait()
        span = [strip_of(step * group + i) for i in range(-1, group + 1)]
        left = pltpu.roll(jnp.stack(span[:group]), 2 * HALO, 2)
        beside = jnp.where(lane < HALO, jnp.stack(span[2:]), left)
        beside = jnp.where(lane < 2 * HALO, beside, 0.0)
        for shift in (16, 32, 64):
            beside = beside + pltpu.roll(beside, shift, 2)
        beside = jnp.where((lane >> 4) == 7 - sublane, beside, 0.0)
        beside = jnp.sum(beside, axis=1, keepdims=True)
        rows = slice(step * group * SPAN, (step + 1) * group * SPAN)
        out = packed.at[rows]
        for i in range(group):
            out[SPAN * i : SPAN * i + TILE, :] = span[i + 1]
            out[SPAN * i + TILE : SPAN * (i + 1), :] = beside[i]
        writes.append(
            pltpu.make_async_copy(packed.at[rows], out_ref.at[rows], sems.at[1, step])
        )
        writes[step].start()
    for write in writes:
        write.wait()


def first_row(block, rows):
    start = jnp.clip(block * CORE_ROWS - TILE, 0, rows - ROWS)
    return pl.multiple_of(start, TILE)


def cut_waves(src_any, rec_any, edges_ref, message_ref, src_ref, rec_ref, sems):
    copies, copy_in = copier(sems)
    copy_in(src_any, src_ref)
    copy_in(rec_any, rec_ref)
    other = 1 - (lax.axis_index("freq") & 1)
    for copy in copies:
        copy.wait()
    fields = (src_ref.at[0, 0], src_ref.at[1, 0], rec_ref.at[0, 0], rec_ref.at[1, 0])
    lane = lanes_of(CORE_ROWS)
    packed = jnp.zeros((CORE_ROWS, LANES), F32)
    for group in range(BLOCKS):
        for part, field in enumerate(fields):
            slot = 4 * group + part
            value = field[group * CORE_ROWS : (group + 1) * CORE_ROWS, :]
            packed = jnp.where((lane >> 3) == slot, lane_roll(value, 8 * slot + 4), packed)
    edges_ref[...] = jnp.where((lane & 7) < 4, lane_roll(packed, -4), lane_roll(packed, 4))
    for b in range(2):
        rows = pl.ds(first_row(2 * b + other, src_ref.shape[2]), ROWS)
        for part, field in enumerate(fields):
            message_ref[4 * b + part] = field[rows, :]


SIN_TERMS = (1.0, -0.166666641831398, 0.008333218283951283, -0.00019823516777250916, 2.643730113049969e-06)
COS_TERMS = (1.0, -0.5, 0.041666656732559204, -0.0013888673856854439, 2.4778757506283e-05, -2.6437069777784927e-07)


def horner(terms, x):
    value = terms[-1]
    for term in terms[-2::-1]:
        value = value * x + term
    return value


def sin_cos(x):
    t = x - 0.7853981633974483
    square = t * t
    sine = t * horner(SIN_TERMS, square)
    cosine = horner(COS_TERMS, square)
    twice = -2.0 * sine
    return 1.0 + twice * sine, twice * cosine


def stepper(waves, speed, coef, omega, first, second, images):
    chunks = ROWS // CHUNK
    guard = jnp.zeros((TILE, LANES), F32)
    for buffer in (first, second):
        for part in range(4):
            buffer[part, 0:GUARD, :] = guard
            buffer[part, GUARD + ROWS :, :] = guard
    images[...] = jnp.zeros_like(images)

    def turn(values, depth, kind, row, freq_row):
        theta = freq_row * speed[kind, depth, pl.ds(row, CHUNK), :]
        sine, cosine = sin_cos(theta)
        src_re, src_im, rec_re, rec_im = values
        return (
            src_re * cosine - src_im * sine,
            src_re * sine + src_im * cosine,
            rec_re * cosine + rec_im * sine,
            rec_im * cosine - rec_re * sine,
        )

    def substep(buffer, depth, kind, row, freq_inverse):
        step = coef[kind, depth, pl.ds(row, CHUNK), :] * freq_inverse
        centers = []
        laps = []
        for part in range(4):
            center = buffer[part, pl.ds(row + GUARD, CHUNK), :]
            up = buffer[part, pl.ds(row + GUARD - 1, CHUNK), :]
            down = buffer[part, pl.ds(row + GUARD + 1, CHUNK), :]
            across = lane_roll(center, 1) + lane_roll(center, LANES - 1)
            centers.append(center)
            laps.append((across + (up + down)) - 4.0 * center)
        src_re, src_im, rec_re, rec_im = centers
        return (
            src_re - step * laps[1],
            src_im + step * laps[0],
            rec_re + step * laps[3],
            rec_im - step * laps[2],
        )

    def store(buffer, row, values):
        for part in range(4):
            buffer[part, pl.ds(row + GUARD, CHUNK), :] = values[part]

    def product(values):
        return values[0] * values[2] + values[1] * values[3]

    def add_image(kind, depth, row, value):
        low, high = max(row, TILE), min(row + CHUNK, TILE + CORE_ROWS)
        if low < high:
            images[kind, depth, low - TILE : high - TILE, :] += value[low - row : high - row, :]

    def item(k, kind):
        freq_row = omega[pl.ds(pl.multiple_of(k * TILE, TILE), 1), :]
        freq_inverse = 1.0 / freq_row

        for j in range(chunks):
            row = j * CHUNK
            values = [waves[k, part, pl.ds(row + GUARD, CHUNK), :] for part in range(4)]
            store(first, row, turn(values, 0, kind, row, freq_row))
        for j in range(chunks):
            store(second, j * CHUNK, substep(first, 0, kind, j * CHUNK, freq_inverse))
        for j in range(chunks):
            row = j * CHUNK
            values = substep(second, 0, kind, row, freq_inverse)
            add_image(kind, 0, row, product(values))
            store(first, row, turn(values, 1, kind, row, freq_row))
        for j in range(chunks):
            store(second, j * CHUNK, substep(first, 1, kind, j * CHUNK, freq_inverse))
        for j in range(chunks):
            values = substep(second, 1, kind, j * CHUNK, freq_inverse)
            add_image(kind, 1, j * CHUNK, product(values))

    return item


def clear_above(waves, items):
    for m in items:
        for part in range(4):
            waves[m, part, GUARD : GUARD + TILE, :] = jnp.zeros((TILE, LANES), F32)


def clear_below(waves, items):
    for m in items:
        for part in range(4):
            rows = slice(GUARD + ROWS - TILE, GUARD + ROWS)
            waves[m, part, rows, :] = jnp.zeros((TILE, LANES), F32)


def copier(sems):
    copies = []

    def copy_in(source, target):
        copy = pltpu.make_async_copy(source, target, sems.at[len(copies)])
        copy.start()
        copies.append(copy)

    return copies, copy_in


def copy_speeds(copy_in, speed_refs, stage, block, core):
    block_rows = SPAN * (CORE_ROWS // TILE)
    mid = pl.multiple_of(block * block_rows, TILE)
    above = pl.multiple_of(jnp.maximum(mid - 16, 0), TILE)
    below = pl.multiple_of(jnp.minimum(mid + block_rows, speed_refs[0].shape[0] - 16), TILE)
    for which, speed_ref in enumerate(speed_refs):
        target = stage.at[core ^ which]
        copy_in(speed_ref.at[pl.ds(above, 16)], target.at[0:16])
        copy_in(speed_ref.at[pl.ds(mid, block_rows)], target.at[16 : 16 + block_rows])
        copy_in(speed_ref.at[pl.ds(below, 16)], target.at[16 + block_rows :])


def copy_waves(copy_in, src_ref, rec_ref, message_ref, waves, block, b, m):
    start = first_row(block, src_ref.shape[2])
    landing = pl.ds(pl.multiple_of(start - block * CORE_ROWS + GUARD + TILE, TILE), ROWS)
    rows = pl.ds(start, ROWS)
    copy_in(src_ref.at[:, 0, rows, :], waves.at[m, 0:2, landing, :])
    copy_in(rec_ref.at[:, 0, rows, :], waves.at[m, 2:4, landing, :])
    copy_in(message_ref.at[pl.ds(4 * b, 4)], waves.at[m + 1, :, landing, :])


def tile_speeds(stage, depth):
    tiles = ROWS // TILE
    return jnp.stack([stage[depth, 7 + SPAN * i : 15 + SPAN * i, :] for i in range(tiles)])


def patch(image, value, b):
    lane = lanes_of(CORE_ROWS)
    image = jnp.where(lane < HALO, pltpu.roll(value, (2 * LANES - 64 * b - 36) & 127, 1), image)
    return jnp.where(
        lane >= LANES - HALO, pltpu.roll(value, (LANES + 100 - 64 * b) & 127, 1), image
    )


def cut_windows(src_ref, rec_ref, message_ref, windows_ref, waves, sems):
    core = lax.axis_index("freq") & 1
    copies, copy_in = copier(sems)
    for b in range(2):
        copy_waves(copy_in, src_ref, rec_ref, message_ref, waves, 2 * b + core, b, 2 * b)
    for copy in copies:
        copy.wait()
    clear_ends(waves, core)
    lane = lanes_of(ROWS)
    place = lane & (WIN - 1)
    for part in range(4):
        own = waves[0, part, GUARD : GUARD + ROWS, :]
        for m in range(1, ITEMS):
            value = lane_roll(waves[m, part, GUARD : GUARD + ROWS, :], WIN * m)
            own = jnp.where((((lane + 16) >> 5) & 3) == m, value, own)
        windows_ref[part] = jnp.where(place < 16, lane_roll(own, 36), lane_roll(own, 28))


def clear_ends(waves, core):
    @pl.when(core == 0)
    def _():
        clear_above(waves, range(2))

    @pl.when(core == 1)
    def _():
        clear_below(waves, range(2, 4))


def march_sent(*refs):
    speed_refs, src_ref, rec_ref, message_ref, halo_refs = refs[:2], *refs[2:5], refs[5:7]
    windows_ref, send_ref, sums_ref = refs[7:10]
    waves, sides, stage, speed, coef, omega, first, second, images, sems = refs[10:]
    freq = lax.axis_index("freq")
    core = freq & 1
    strip = lax.axis_index("strip")
    strips = lax.axis_size("strip")
    copies, copy_in = copier(sems)
    for b in range(2):
        copy_speeds(copy_in, speed_refs, stage.at[b], 2 * b + core, core)
    speed_count = len(copies)
    sent = 1 - (freq >> 1)
    sent_block = 2 * sent + core
    copy_waves(copy_in, src_ref, rec_ref, message_ref, waves, sent_block, sent, 0)
    for k in range(2):
        copy_in(halo_refs[k], sides.at[k])
    copy_in(windows_ref, waves.at[2, :, GUARD : GUARD + ROWS, :])

    item = stepper(waves, speed, coef, omega, first, second, images)
    for copy in copies[:speed_count]:
        copy.wait()
    tiles = ROWS // TILE
    dims = (tiles, TILE, LANES)
    lane = lax.broadcasted_iota(jnp.int32, dims, 2)
    place = lane & (WIN - 1)
    tile = lax.broadcasted_iota(jnp.int32, dims, 0)
    on_grid = jnp.logical_not(
        ((place < 4) & (strip == 0)) | ((place >= 28) & (strip == strips - 1))
    )
    sent_live = jnp.logical_not(
        ((tile == 0) & (sent_block == 0)) | ((tile == tiles - 1) & (sent_block == BLOCKS - 1))
    )
    for depth in range(2):
        window = jnp.zeros(dims, F32)
        window_live = place < 0
        for b in range(2):
            block = 2 * b + core
            live = jnp.logical_not(
                ((tile == 0) & (block == 0)) | ((tile == tiles - 1) & (block == BLOCKS - 1))
            )
            here = tile_speeds(stage.at[b], depth)
            beside = jnp.stack(
                [
                    jnp.broadcast_to(
                        stage[b, depth, 15 + SPAN * i : 16 + SPAN * i, :], (TILE, LANES)
                    )
                    for i in range(tiles)
                ]
            )
            beside = pltpu.roll(beside, 0, 2, stride=16, stride_axis=1)
            base = 64 * b

            def lanes_in(low, high):
                return (lane >= base + low) & (lane < base + high)

            window = jnp.where(
                lanes_in(16, 28), pltpu.roll(here, (base + 28) % LANES, 2), window
            )
            window = jnp.where(
                lanes_in(28, 36), pltpu.roll(beside, (base + 44) % LANES, 2), window
            )
            window = jnp.where(
                lanes_in(36, 48), pltpu.roll(here, (base + 36) % LANES, 2), window
            )
            window_live = window_live | (live & ((((lane + 112) >> 6) & 1) == b))
        window = window + pltpu.roll(window, WIN, 2)
        here = tile_speeds(stage.at[sent], depth)
        speed[0, depth] = (half_depth / here).reshape(ROWS, LANES)
        coef[0, depth] = jnp.where(sent_live, fd_coef * here, 0.0).reshape(ROWS, LANES)
        speed[1, depth] = (half_depth / window).reshape(ROWS, LANES)
        coef[1, depth] = jnp.where(
            on_grid & window_live, fd_coef * window, 0.0
        ).reshape(ROWS, LANES)

    for copy in copies[speed_count:]:
        copy.wait()

    @pl.when(sent_block == 0)
    def _():
        clear_above(waves, range(2))

    @pl.when(sent_block == BLOCKS - 1)
    def _():
        clear_below(waves, range(2))

    def turned(k, low, high, shift):
        return pltpu.roll(sides[k, low:high, :], (WIN * (shift - core)) & (LANES - 1), 1)

    def pick(low, high, shift):
        odd = ((lanes_of(high - low) >> 5) & 1) == 1
        return jnp.where(odd, turned(1, low, high, shift + 1), turned(0, low, high, shift))

    tile_lane = lanes_of(TILE)
    above = pick(CORE_ROWS - TILE, CORE_ROWS, 1)
    above = jnp.where((tile_lane < 2 * WIN) & (core == 0), 0.0, above)
    below = pick(0, TILE, LANES // WIN - 1)
    below = jnp.where((tile_lane >= 2 * WIN) & (core == 1), 0.0, below)
    beside = jnp.concatenate([above, pick(0, CORE_ROWS, 0), below])
    place = lanes_of(ROWS) & (WIN - 1)
    halo = (place < 4) | (place >= 28)
    for part in range(4):
        window = waves[2, part, GUARD : GUARD + ROWS, :]
        waves[2, part, GUARD : GUARD + ROWS, :] = jnp.where(
            halo, lane_roll(beside, 28 - 8 * part), window
        )
    rows = [sides[k, CORE_ROWS : CORE_ROWS + TILE, :] for k in range(2)]
    odd = (((tile_lane + 112) >> 5) & 1) == 1
    for k in range(2):
        omega[k * TILE : (k + 1) * TILE, :] = rows[k]
    omega[2 * TILE :, :] = jnp.where(odd, rows[1], rows[0])

    def step(k, carry):
        item(k, k >> 1)
        return carry

    lax.fori_loop(0, 3, step, 0)
    for depth in range(2):
        value = images[1, depth]
        value = value + lane_roll(value, -WIN)
        sums_ref[depth] = value
        send_ref[depth] = patch(images[0, depth], value, sent)


def march_kept(*refs):
    speed_refs, src_ref, rec_ref, message_ref, halo_refs = refs[:2], *refs[2:5], refs[5:7]
    sums_ref, image_ref = refs[7:9]
    waves, stage, speed, coef, omega, first, second, images, sems = refs[9:]
    freq = lax.axis_index("freq")
    core = freq & 1
    b = freq >> 1
    copies, copy_in = copier(sems)
    copy_speeds(copy_in, speed_refs, stage, freq, core)
    copy_waves(copy_in, src_ref, rec_ref, message_ref, waves, freq, b, 0)
    for k in range(2):
        copy_in(
            halo_refs[k].at[CORE_ROWS : CORE_ROWS + TILE], omega.at[k * TILE : (k + 1) * TILE]
        )
    item = stepper(waves, speed, coef, omega, first, second, images)
    for copy in copies:
        copy.wait()
    tiles = ROWS // TILE
    tile = lax.broadcasted_iota(jnp.int32, (tiles, TILE, LANES), 0)
    live = jnp.logical_not(
        ((tile == 0) & (freq == 0)) | ((tile == tiles - 1) & (freq == BLOCKS - 1))
    )
    for depth in range(2):
        here = tile_speeds(stage, depth)
        speed[0, depth] = (half_depth / here).reshape(ROWS, LANES)
        coef[0, depth] = jnp.where(live, fd_coef * here, 0.0).reshape(ROWS, LANES)

    @pl.when(freq == 0)
    def _():
        clear_above(waves, range(2))

    @pl.when(freq == BLOCKS - 1)
    def _():
        clear_below(waves, range(2))

    def step(k, carry):
        item(k, 0)
        return carry

    lax.fori_loop(0, 2, step, 0)
    for depth in range(2):
        image_ref[depth] = patch(images[0, depth], sums_ref[depth], b)


SMALL = pltpu.CompilerParams(vmem_limit_bytes=16 * 1024 * 1024)


def shape(*dims):
    return jax.ShapeDtypeStruct(dims, F32)


def shards(source, receiver, velocity, omega):
    strips = lax.axis_size("strip")
    freqs = lax.axis_size("freq")
    vmem = pl.BlockSpec(memory_space=pltpu.VMEM)
    anywhere = pl.BlockSpec(memory_space=pl.ANY)

    def across(x, k):
        return lax.ppermute(x, "freq", [(i, i ^ k) for i in range(freqs)])

    packed = pl.pallas_call(
        pack_speed,
        out_shape=shape(SPAN * strips, LANES),
        in_specs=[anywhere],
        out_specs=anywhere,
        scratch_shapes=[
            pltpu.VMEM((TILE, strips * LANES), F32),
            pltpu.VMEM((SPAN * strips, LANES), F32),
            pltpu.SemaphoreType.DMA((2, GROUPS)),
        ],
    )(velocity)
    speeds = lax.all_to_all(
        packed.reshape(strips, 1, SPAN * LANES), "strip", split_axis=0, concat_axis=0, tiled=True
    ).reshape(SPAN * strips, LANES)
    other_speeds = across(speeds, 1)

    edges, message = pl.pallas_call(
        cut_waves,
        out_shape=[shape(CORE_ROWS, LANES), shape(8, ROWS, LANES)],
        in_specs=[anywhere, anywhere],
        out_specs=[vmem, vmem],
        scratch_shapes=[pltpu.VMEM(source.shape, F32)] * 2 + [pltpu.SemaphoreType.DMA((2,))],
        compiler_params=SMALL,
    )(source, receiver)
    def swap(x, pairs):
        return lax.ppermute(x, "strip", [p for i, j in pairs for p in ((i, j), (j, i))])

    with_far = swap(edges, [(i, i + 1) for i in range(1, strips - 1, 2)])
    with_near = swap(edges, [(i, i + 1) for i in range(0, strips, 2)])
    message = across(message, 1)
    parity = lax.axis_index("strip") & 1
    from_near = (((lanes_of(CORE_ROWS) >> 2) ^ parity) & 1) == 0
    halos = jnp.concatenate(
        [
            jnp.where(from_near, with_near, with_far),
            jnp.broadcast_to(omega[:, None], (TILE, LANES)),
        ]
    )

    windows = pl.pallas_call(
        cut_windows,
        out_shape=shape(4, ROWS, LANES),
        in_specs=[anywhere] * 3,
        out_specs=vmem,
        scratch_shapes=[
            pltpu.VMEM((ITEMS, 4, ROWS + 2 * GUARD, LANES), F32),
            pltpu.SemaphoreType.DMA((6,)),
        ],
        compiler_params=SMALL,
    )(source, receiver, message)
    inputs = (speeds, other_speeds, source, receiver, message, halos, across(halos, 1))

    def scratch(items, kinds):
        return [
            pltpu.VMEM((kinds, 2, ROWS, LANES), F32),
            pltpu.VMEM((kinds, 2, ROWS, LANES), F32),
            pltpu.VMEM((items * TILE, LANES), F32),
            pltpu.VMEM((4, ROWS + 2 * GUARD, LANES), F32),
            pltpu.VMEM((4, ROWS + 2 * GUARD, LANES), F32),
            pltpu.VMEM((kinds, 2, CORE_ROWS, LANES), F32),
            pltpu.SemaphoreType.DMA((21,)),
        ]

    stage_rows = 32 + SPAN * CORE_ROWS // TILE
    send, sums = pl.pallas_call(
        march_sent,
        out_shape=[shape(2, CORE_ROWS, LANES)] * 2,
        in_specs=[anywhere] * 8,
        out_specs=[vmem] * 2,
        scratch_shapes=[
            pltpu.VMEM((3, 4, ROWS + 2 * GUARD, LANES), F32),
            pltpu.VMEM((2, CORE_ROWS + TILE, LANES), F32),
            pltpu.VMEM((2, 2, stage_rows, LANES), F32),
        ]
        + scratch(3, 2),
        compiler_params=SMALL,
    )(*inputs, windows)
    received = across(send, 2)
    kept = pl.pallas_call(
        march_kept,
        out_shape=shape(2, CORE_ROWS, LANES),
        in_specs=[anywhere] * 7 + [vmem],
        out_specs=vmem,
        scratch_shapes=[
            pltpu.VMEM((2, 4, ROWS + 2 * GUARD, LANES), F32),
            pltpu.VMEM((2, stage_rows, LANES), F32),
        ]
        + scratch(2, 1),
        compiler_params=SMALL,
    )(*inputs, sums)
    return kept + received


def solution(mesh):
    return jax.shard_map(
        shards,
        mesh=mesh,
        in_specs=(
            P(None, "freq", None, "strip"),
            P(None, "freq", None, "strip"),
            P(None, "strip", None),
            P("freq"),
        ),
        out_specs=P(None, "freq", "strip"),
        check_vma=False,
    )
```

```python
import functools

import jax
import jax.numpy as jnp
from jax import lax
from jax.experimental import pallas as pl
from jax.experimental.pallas import tpu as pltpu
from jax.sharding import PartitionSpec as P

BLOCKS = 4
ITEMS = 4
LANES = 128
TILE = 8
WIN = 32
HALO = 4
CORE_ROWS = 128
ROWS = CORE_ROWS + 2 * TILE
GUARD = TILE
CHUNK = 72
SPAN = 9
GROUPS = 1

phase_depth = 2.0
fd_coef = 0.03

F32 = jnp.float32


def lanes_of(rows):
    return lax.broadcasted_iota(jnp.int32, (rows, LANES), 1)


def lane_roll(x, shift):
    return pltpu.roll(x, shift % LANES, 1)


def pack_speed(vel_ref, out_ref, held, packed, sems):
    core = lax.axis_index("freq") & 1
    strips = vel_ref.shape[2] // LANES
    group = strips // GROUPS
    width = group * LANES
    reads = []
    for step in range(GROUPS):
        columns = slice(step * width, (step + 1) * width)
        reads.append(
            pltpu.make_async_copy(
                vel_ref.at[core, :, columns], held.at[:, columns], sems.at[0, step]
            )
        )
        reads[step].start()
    dims = (group, TILE, LANES)
    lane = lax.broadcasted_iota(jnp.int32, dims, 2)
    sublane = lax.broadcasted_iota(jnp.int32, dims, 1)

    def strip_of(strip):
        strip = min(max(strip, 0), strips - 1)
        return held[:, strip * LANES : (strip + 1) * LANES]

    writes = []
    reads[0].wait()
    for step in range(GROUPS):
        if step + 1 < GROUPS:
            reads[step + 1].wait()
        span = [strip_of(step * group + i) for i in range(-1, group + 1)]
        left = pltpu.roll(jnp.stack(span[:group]), 2 * HALO, 2)
        beside = jnp.where(lane < HALO, jnp.stack(span[2:]), left)
        beside = jnp.where(lane < 2 * HALO, beside, 0.0)
        for shift in (16, 32, 64):
            beside = beside + pltpu.roll(beside, shift, 2)
        beside = jnp.where((lane >> 4) == 7 - sublane, beside, 0.0)
        beside = jnp.sum(beside, axis=1, keepdims=True)
        rows = slice(step * group * SPAN, (step + 1) * group * SPAN)
        out = packed.at[rows]
        for i in range(group):
            out[SPAN * i : SPAN * i + TILE, :] = span[i + 1]
            out[SPAN * i + TILE : SPAN * (i + 1), :] = beside[i]
        writes.append(
            pltpu.make_async_copy(packed.at[rows], out_ref.at[rows], sems.at[1, step])
        )
        writes[step].start()
    for write in writes:
        write.wait()


def first_row(block, rows):
    start = jnp.clip(block * CORE_ROWS - TILE, 0, rows - ROWS)
    return pl.multiple_of(start, TILE)


def cut_waves(src_any, rec_any, edges_ref, message_ref, src_ref, rec_ref, sems):
    copies, copy_in = copier(sems)
    copy_in(src_any, src_ref)
    copy_in(rec_any, rec_ref)
    other = 1 - (lax.axis_index("freq") & 1)
    for copy in copies:
        copy.wait()
    fields = (src_ref.at[0, 0], src_ref.at[1, 0], rec_ref.at[0, 0], rec_ref.at[1, 0])
    lane = lanes_of(CORE_ROWS)
    packed = jnp.zeros((CORE_ROWS, LANES), F32)
    for group in range(BLOCKS):
        for part, field in enumerate(fields):
            slot = 4 * group + part
            value = field[group * CORE_ROWS : (group + 1) * CORE_ROWS, :]
            packed = jnp.where((lane >> 3) == slot, lane_roll(value, 8 * slot + 4), packed)
    edges_ref[...] = jnp.where((lane & 7) < 4, lane_roll(packed, -4), lane_roll(packed, 4))
    for b in range(2):
        rows = pl.ds(first_row(2 * b + other, src_ref.shape[2]), ROWS)
        for part, field in enumerate(fields):
            message_ref[4 * b + part] = field[rows, :]


SIN_TERMS = (1.0, -0.166666641831398, 0.008333218283951283, -0.00019823516777250916, 2.643730113049969e-06)
COS_TERMS = (1.0, -0.5, 0.041666656732559204, -0.0013888673856854439, 2.4778757506283e-05, -2.6437069777784927e-07)


def horner(terms, x):
    value = terms[-1]
    for term in terms[-2::-1]:
        value = value * x + term
    return value


def sin_cos(x):
    t = 0.5 * x - 0.7853981633974483
    square = t * t
    sine = t * horner(SIN_TERMS, square)
    cosine = horner(COS_TERMS, square)
    twice = -2.0 * sine
    return 1.0 + twice * sine, twice * cosine


def stepper(waves, speed, coef, omega, first, second, images):
    chunks = ROWS // CHUNK
    guard = jnp.zeros((TILE, LANES), F32)
    for buffer in (first, second):
        for part in range(4):
            buffer[part, 0:GUARD, :] = guard
            buffer[part, GUARD + ROWS :, :] = guard
    images[...] = jnp.zeros_like(images)

    def turn(values, depth, kind, row, freq_row):
        theta = freq_row * speed[kind, depth, pl.ds(row, CHUNK), :]
        sine, cosine = sin_cos(theta)
        src_re, src_im, rec_re, rec_im = values
        return (
            src_re * cosine - src_im * sine,
            src_re * sine + src_im * cosine,
            rec_re * cosine + rec_im * sine,
            rec_im * cosine - rec_re * sine,
        )

    def substep(buffer, depth, kind, row, freq_inverse):
        step = coef[kind, depth, pl.ds(row, CHUNK), :] * freq_inverse
        centers = []
        laps = []
        for part in range(4):
            center = buffer[part, pl.ds(row + GUARD, CHUNK), :]
            up = buffer[part, pl.ds(row + GUARD - 1, CHUNK), :]
            down = buffer[part, pl.ds(row + GUARD + 1, CHUNK), :]
            across = lane_roll(center, 1) + lane_roll(center, LANES - 1)
            centers.append(center)
            laps.append((across + (up + down)) - 4.0 * center)
        src_re, src_im, rec_re, rec_im = centers
        return (
            src_re - step * laps[1],
            src_im + step * laps[0],
            rec_re + step * laps[3],
            rec_im - step * laps[2],
        )

    def store(buffer, row, values):
        for part in range(4):
            buffer[part, pl.ds(row + GUARD, CHUNK), :] = values[part]

    def product(values):
        return values[0] * values[2] + values[1] * values[3]

    def add_image(kind, depth, row, value):
        low, high = max(row, TILE), min(row + CHUNK, TILE + CORE_ROWS)
        if low < high:
            images[kind, depth, low - TILE : high - TILE, :] += value[low - row : high - row, :]

    def item(k, kind):
        freq_row = omega[pl.ds(pl.multiple_of(k * TILE, TILE), 1), :]
        freq_inverse = 1.0 / freq_row

        for j in range(chunks):
            row = j * CHUNK
            values = [waves[k, part, pl.ds(row + GUARD, CHUNK), :] for part in range(4)]
            store(first, row, turn(values, 0, kind, row, freq_row))
        for j in range(chunks):
            store(second, j * CHUNK, substep(first, 0, kind, j * CHUNK, freq_inverse))
        for j in range(chunks):
            row = j * CHUNK
            values = substep(second, 0, kind, row, freq_inverse)
            add_image(kind, 0, row, product(values))
            store(first, row, turn(values, 1, kind, row, freq_row))
        for j in range(chunks):
            store(second, j * CHUNK, substep(first, 1, kind, j * CHUNK, freq_inverse))
        for j in range(chunks):
            values = substep(second, 1, kind, j * CHUNK, freq_inverse)
            add_image(kind, 1, j * CHUNK, product(values))

    return item


def clear_above(waves, items):
    for m in items:
        for part in range(4):
            waves[m, part, GUARD : GUARD + TILE, :] = jnp.zeros((TILE, LANES), F32)


def clear_below(waves, items):
    for m in items:
        for part in range(4):
            rows = slice(GUARD + ROWS - TILE, GUARD + ROWS)
            waves[m, part, rows, :] = jnp.zeros((TILE, LANES), F32)


def copier(sems):
    copies = []

    def copy_in(source, target):
        copy = pltpu.make_async_copy(source, target, sems.at[len(copies)])
        copy.start()
        copies.append(copy)

    return copies, copy_in


def copy_speeds(copy_in, speed_refs, stage, block, core):
    block_rows = SPAN * (CORE_ROWS // TILE)
    mid = pl.multiple_of(block * block_rows, TILE)
    above = pl.multiple_of(jnp.maximum(mid - 16, 0), TILE)
    below = pl.multiple_of(jnp.minimum(mid + block_rows, speed_refs[0].shape[0] - 16), TILE)
    for which, speed_ref in enumerate(speed_refs):
        target = stage.at[core ^ which]
        copy_in(speed_ref.at[pl.ds(above, 16)], target.at[0:16])
        copy_in(speed_ref.at[pl.ds(mid, block_rows)], target.at[16 : 16 + block_rows])
        copy_in(speed_ref.at[pl.ds(below, 16)], target.at[16 + block_rows :])


def copy_waves(copy_in, src_ref, rec_ref, message_ref, waves, block, b, m):
    start = first_row(block, src_ref.shape[2])
    landing = pl.ds(pl.multiple_of(start - block * CORE_ROWS + GUARD + TILE, TILE), ROWS)
    rows = pl.ds(start, ROWS)
    copy_in(src_ref.at[:, 0, rows, :], waves.at[m, 0:2, landing, :])
    copy_in(rec_ref.at[:, 0, rows, :], waves.at[m, 2:4, landing, :])
    copy_in(message_ref.at[pl.ds(4 * b, 4)], waves.at[m + 1, :, landing, :])


def tile_speeds(stage, depth):
    tiles = ROWS // TILE
    return jnp.stack([stage[depth, 7 + SPAN * i : 15 + SPAN * i, :] for i in range(tiles)])


def patch(image, value, b):
    lane = lanes_of(CORE_ROWS)
    image = jnp.where(lane < HALO, pltpu.roll(value, (2 * LANES - 64 * b - 36) & 127, 1), image)
    return jnp.where(
        lane >= LANES - HALO, pltpu.roll(value, (LANES + 100 - 64 * b) & 127, 1), image
    )


def cut_windows(src_ref, rec_ref, message_ref, windows_ref, waves, sems):
    core = lax.axis_index("freq") & 1
    copies, copy_in = copier(sems)
    for b in range(2):
        copy_waves(copy_in, src_ref, rec_ref, message_ref, waves, 2 * b + core, b, 2 * b)
    for copy in copies:
        copy.wait()
    clear_ends(waves, core)
    lane = lanes_of(ROWS)
    place = lane & (WIN - 1)
    for part in range(4):
        own = waves[0, part, GUARD : GUARD + ROWS, :]
        for m in range(1, ITEMS):
            value = lane_roll(waves[m, part, GUARD : GUARD + ROWS, :], WIN * m)
            own = jnp.where((((lane + 16) >> 5) & 3) == m, value, own)
        windows_ref[part] = jnp.where(place < 16, lane_roll(own, 36), lane_roll(own, 28))


def clear_ends(waves, core):
    @pl.when(core == 0)
    def _():
        clear_above(waves, range(2))

    @pl.when(core == 1)
    def _():
        clear_below(waves, range(2, 4))


def march_sent(*refs):
    speed_refs, src_ref, rec_ref, message_ref, halo_refs = refs[:2], *refs[2:5], refs[5:7]
    windows_ref, send_ref, sums_ref = refs[7:10]
    waves, sides, stage, speed, coef, omega, first, second, images, sems = refs[10:]
    freq = lax.axis_index("freq")
    core = freq & 1
    strip = lax.axis_index("strip")
    strips = lax.axis_size("strip")
    copies, copy_in = copier(sems)
    for b in range(2):
        copy_speeds(copy_in, speed_refs, stage.at[b], 2 * b + core, core)
    speed_count = len(copies)
    sent = 1 - (freq >> 1)
    sent_block = 2 * sent + core
    copy_waves(copy_in, src_ref, rec_ref, message_ref, waves, sent_block, sent, 0)
    for k in range(2):
        copy_in(halo_refs[k], sides.at[k])
    copy_in(windows_ref, waves.at[2, :, GUARD : GUARD + ROWS, :])

    item = stepper(waves, speed, coef, omega, first, second, images)
    for copy in copies[:speed_count]:
        copy.wait()
    tiles = ROWS // TILE
    dims = (tiles, TILE, LANES)
    lane = lax.broadcasted_iota(jnp.int32, dims, 2)
    place = lane & (WIN - 1)
    tile = lax.broadcasted_iota(jnp.int32, dims, 0)
    on_grid = jnp.logical_not(
        ((place < 4) & (strip == 0)) | ((place >= 28) & (strip == strips - 1))
    )
    sent_live = jnp.logical_not(
        ((tile == 0) & (sent_block == 0)) | ((tile == tiles - 1) & (sent_block == BLOCKS - 1))
    )
    for depth in range(2):
        window = jnp.zeros(dims, F32)
        window_live = place < 0
        for b in range(2):
            block = 2 * b + core
            live = jnp.logical_not(
                ((tile == 0) & (block == 0)) | ((tile == tiles - 1) & (block == BLOCKS - 1))
            )
            here = tile_speeds(stage.at[b], depth)
            beside = jnp.stack(
                [
                    jnp.broadcast_to(
                        stage[b, depth, 15 + SPAN * i : 16 + SPAN * i, :], (TILE, LANES)
                    )
                    for i in range(tiles)
                ]
            )
            beside = pltpu.roll(beside, 0, 2, stride=16, stride_axis=1)
            base = 64 * b

            def lanes_in(low, high):
                return (lane >= base + low) & (lane < base + high)

            window = jnp.where(
                lanes_in(16, 28), pltpu.roll(here, (base + 28) % LANES, 2), window
            )
            window = jnp.where(
                lanes_in(28, 36), pltpu.roll(beside, (base + 44) % LANES, 2), window
            )
            window = jnp.where(
                lanes_in(36, 48), pltpu.roll(here, (base + 36) % LANES, 2), window
            )
            window_live = window_live | (live & ((((lane + 112) >> 6) & 1) == b))
        window = window + pltpu.roll(window, WIN, 2)
        here = tile_speeds(stage.at[sent], depth)
        speed[0, depth] = (phase_depth / here).reshape(ROWS, LANES)
        coef[0, depth] = jnp.where(sent_live, fd_coef * here, 0.0).reshape(ROWS, LANES)
        speed[1, depth] = (phase_depth / window).reshape(ROWS, LANES)
        coef[1, depth] = jnp.where(
            on_grid & window_live, fd_coef * window, 0.0
        ).reshape(ROWS, LANES)

    for copy in copies[speed_count:]:
        copy.wait()

    @pl.when(sent_block == 0)
    def _():
        clear_above(waves, range(2))

    @pl.when(sent_block == BLOCKS - 1)
    def _():
        clear_below(waves, range(2))

    def turned(k, low, high, shift):
        return pltpu.roll(sides[k, low:high, :], (WIN * (shift - core)) & (LANES - 1), 1)

    def pick(low, high, shift):
        odd = ((lanes_of(high - low) >> 5) & 1) == 1
        return jnp.where(odd, turned(1, low, high, shift + 1), turned(0, low, high, shift))

    tile_lane = lanes_of(TILE)
    above = pick(CORE_ROWS - TILE, CORE_ROWS, 1)
    above = jnp.where((tile_lane < 2 * WIN) & (core == 0), 0.0, above)
    below = pick(0, TILE, LANES // WIN - 1)
    below = jnp.where((tile_lane >= 2 * WIN) & (core == 1), 0.0, below)
    beside = jnp.concatenate([above, pick(0, CORE_ROWS, 0), below])
    place = lanes_of(ROWS) & (WIN - 1)
    halo = (place < 4) | (place >= 28)
    for part in range(4):
        window = waves[2, part, GUARD : GUARD + ROWS, :]
        waves[2, part, GUARD : GUARD + ROWS, :] = jnp.where(
            halo, lane_roll(beside, 28 - 8 * part), window
        )
    rows = [sides[k, CORE_ROWS : CORE_ROWS + TILE, :] for k in range(2)]
    odd = (((tile_lane + 112) >> 5) & 1) == 1
    for k in range(2):
        omega[k * TILE : (k + 1) * TILE, :] = rows[k]
    omega[2 * TILE :, :] = jnp.where(odd, rows[1], rows[0])

    def step(k, carry):
        item(k, k >> 1)
        return carry

    lax.fori_loop(0, 3, step, 0)
    for depth in range(2):
        value = images[1, depth]
        value = value + lane_roll(value, -WIN)
        sums_ref[depth] = value
        send_ref[depth] = patch(images[0, depth], value, sent)


def march_kept(*refs):
    speed_refs, src_ref, rec_ref, message_ref, halo_refs = refs[:2], *refs[2:5], refs[5:7]
    sums_ref, image_ref = refs[7:9]
    waves, stage, speed, coef, omega, first, second, images, sems = refs[9:]
    freq = lax.axis_index("freq")
    core = freq & 1
    b = freq >> 1
    copies, copy_in = copier(sems)
    copy_speeds(copy_in, speed_refs, stage, freq, core)
    copy_waves(copy_in, src_ref, rec_ref, message_ref, waves, freq, b, 0)
    for k in range(2):
        copy_in(
            halo_refs[k].at[CORE_ROWS : CORE_ROWS + TILE], omega.at[k * TILE : (k + 1) * TILE]
        )
    item = stepper(waves, speed, coef, omega, first, second, images)
    for copy in copies:
        copy.wait()
    tiles = ROWS // TILE
    tile = lax.broadcasted_iota(jnp.int32, (tiles, TILE, LANES), 0)
    live = jnp.logical_not(
        ((tile == 0) & (freq == 0)) | ((tile == tiles - 1) & (freq == BLOCKS - 1))
    )
    for depth in range(2):
        here = tile_speeds(stage, depth)
        speed[0, depth] = (phase_depth / here).reshape(ROWS, LANES)
        coef[0, depth] = jnp.where(live, fd_coef * here, 0.0).reshape(ROWS, LANES)

    @pl.when(freq == 0)
    def _():
        clear_above(waves, range(2))

    @pl.when(freq == BLOCKS - 1)
    def _():
        clear_below(waves, range(2))

    def step(k, carry):
        item(k, 0)
        return carry

    lax.fori_loop(0, 2, step, 0)
    for depth in range(2):
        image_ref[depth] = patch(images[0, depth], sums_ref[depth], b)


SMALL = pltpu.CompilerParams(vmem_limit_bytes=16 * 1024 * 1024)


def shape(*dims):
    return jax.ShapeDtypeStruct(dims, F32)


def shards(source, receiver, velocity, omega):
    strips = lax.axis_size("strip")
    freqs = lax.axis_size("freq")
    vmem = pl.BlockSpec(memory_space=pltpu.VMEM)
    anywhere = pl.BlockSpec(memory_space=pl.ANY)

    def across(x, k):
        return lax.ppermute(x, "freq", [(i, i ^ k) for i in range(freqs)])

    packed = pl.pallas_call(
        pack_speed,
        out_shape=shape(SPAN * strips, LANES),
        in_specs=[anywhere],
        out_specs=anywhere,
        scratch_shapes=[
            pltpu.VMEM((TILE, strips * LANES), F32),
            pltpu.VMEM((SPAN * strips, LANES), F32),
            pltpu.SemaphoreType.DMA((2, GROUPS)),
        ],
    )(velocity)
    speeds = lax.all_to_all(
        packed.reshape(strips, 1, SPAN * LANES), "strip", split_axis=0, concat_axis=0, tiled=True
    ).reshape(SPAN * strips, LANES)
    other_speeds = across(speeds, 1)

    edges, message = pl.pallas_call(
        cut_waves,
        out_shape=[shape(CORE_ROWS, LANES), shape(8, ROWS, LANES)],
        in_specs=[anywhere, anywhere],
        out_specs=[vmem, vmem],
        scratch_shapes=[pltpu.VMEM(source.shape, F32)] * 2 + [pltpu.SemaphoreType.DMA((2,))],
        compiler_params=SMALL,
    )(source, receiver)
    def swap(x, pairs):
        return lax.ppermute(x, "strip", [p for i, j in pairs for p in ((i, j), (j, i))])

    with_far = swap(edges, [(i, i + 1) for i in range(1, strips - 1, 2)])
    with_near = swap(edges, [(i, i + 1) for i in range(0, strips, 2)])
    message = across(message, 1)
    parity = lax.axis_index("strip") & 1
    from_near = (((lanes_of(CORE_ROWS) >> 2) ^ parity) & 1) == 0
    halos = jnp.concatenate(
        [
            jnp.where(from_near, with_near, with_far),
            jnp.broadcast_to(omega[:, None], (TILE, LANES)),
        ]
    )

    windows = pl.pallas_call(
        cut_windows,
        out_shape=shape(4, ROWS, LANES),
        in_specs=[anywhere] * 3,
        out_specs=vmem,
        scratch_shapes=[
            pltpu.VMEM((ITEMS, 4, ROWS + 2 * GUARD, LANES), F32),
            pltpu.SemaphoreType.DMA((6,)),
        ],
        compiler_params=SMALL,
    )(source, receiver, message)
    inputs = (speeds, other_speeds, source, receiver, message, halos, across(halos, 1))

    def scratch(items, kinds):
        return [
            pltpu.VMEM((kinds, 2, ROWS, LANES), F32),
            pltpu.VMEM((kinds, 2, ROWS, LANES), F32),
            pltpu.VMEM((items * TILE, LANES), F32),
            pltpu.VMEM((4, ROWS + 2 * GUARD, LANES), F32),
            pltpu.VMEM((4, ROWS + 2 * GUARD, LANES), F32),
            pltpu.VMEM((kinds, 2, CORE_ROWS, LANES), F32),
            pltpu.SemaphoreType.DMA((21,)),
        ]

    stage_rows = 32 + SPAN * CORE_ROWS // TILE
    send, sums = pl.pallas_call(
        march_sent,
        out_shape=[shape(2, CORE_ROWS, LANES)] * 2,
        in_specs=[anywhere] * 8,
        out_specs=[vmem] * 2,
        scratch_shapes=[
            pltpu.VMEM((3, 4, ROWS + 2 * GUARD, LANES), F32),
            pltpu.VMEM((2, CORE_ROWS + TILE, LANES), F32),
            pltpu.VMEM((2, 2, stage_rows, LANES), F32),
        ]
        + scratch(3, 2),
        compiler_params=SMALL,
    )(*inputs, windows)
    received = across(send, 2)
    kept = pl.pallas_call(
        march_kept,
        out_shape=shape(2, CORE_ROWS, LANES),
        in_specs=[anywhere] * 7 + [vmem],
        out_specs=vmem,
        scratch_shapes=[
            pltpu.VMEM((2, 4, ROWS + 2 * GUARD, LANES), F32),
            pltpu.VMEM((2, stage_rows, LANES), F32),
        ]
        + scratch(2, 1),
        compiler_params=SMALL,
    )(*inputs, sums)
    return kept + received


def solution(mesh):
    return jax.shard_map(
        shards,
        mesh=mesh,
        in_specs=(
            P(None, "freq", None, "strip"),
            P(None, "freq", None, "strip"),
            P(None, "strip", None),
            P("freq"),
        ),
        out_specs=P(None, "freq", "strip"),
        check_vma=False,
    )
```
